32 devices in a mesh: band: 4 (over x, core), mesh: 8 (over z, y).
Axes of the slice: x: 2, y: 2, z: 4, core: 2. Of those that a mesh axis runs over, the one named last changes fastest.
Arguments:
- grid_vars: bfloat16 [32768, 227], P(('band', 'mesh')), may hold values from -6 to 6
- mesh_latent: bfloat16 [10240, 512], P(('band', 'mesh')), may hold values from -6 to 6
- cotangent: bfloat16 [10240, 512], P(('band', 'mesh')), may hold values from -6 to 6
- edge_grid: int32 [131072], P(('band', 'mesh')), may hold values from 0 to 32767, as said below
- edge_mesh: int32 [131072], P(('band', 'mesh')), may hold values from 0 to 10239, as said below
- w_in: bfloat16 [227, 512], replicated, may hold values from -0.375 to 0.375
- b_in: float32 [512], replicated, may hold values from -4 to 4
- w_out: bfloat16 [512, 512], replicated, may hold values from -0.25 to 0.25
- norm_gain: float32 [512], replicated, may hold values from 0.1 to 1.9
- u_grid: bfloat16 [512, 512], replicated, may hold values from -0.25 to 0.25
- u_mesh: bfloat16 [512, 512], replicated, may hold values from -0.25 to 0.25
- b_edge: float32 [512], replicated, may hold values from -4 to 4
- w_edge: bfloat16 [512, 512], replicated, may hold values from -0.25 to 0.25
- w_self: bfloat16 [512, 512], replicated, may hold values from -0.25 to 0.25
- w_agg: bfloat16 [512, 512], replicated, may hold values from -0.1875 to 0.1875
- b_node: float32 [512], replicated, may hold values from -4 to 4
- w_node_out: bfloat16 [512, 512], replicated, may hold values from -0.25 to 0.25
Outputs:
- mesh_out: bfloat16 [10240, 512], P(('band', 'mesh'))
- grad_mesh: bfloat16 [10240, 512], P(('band', 'mesh'))
- grad_edge: float32 [512, 512], replicated
- grad_ugrid: float32 [512, 512], replicated
- grad_umesh: float32 [512, 512], replicated
The draws below stay inside these ranges and needn't reach their ends.
Inputs may be any that keep to these rules, and one draw needn't show every extreme that they name: `edge_grid`: the edges of one device (aligned blocks of 4096) have grid nodes among that device's 1024 grid nodes. `edge_mesh`: the edges of one device have mesh nodes among the 2560 mesh nodes of the device's band (the nodes of the 8 devices of that band), in nondecreasing order within the device's block. One device's edges reach at most 48 distinct mesh nodes owned by any one device (blocks of 320 mesh nodes); this most is reached in every draw.
All inputs are finite; a program needn't handle non-finite values.
Results may differ from the reference program's by a relative error of at most 0.013.
The reference program's roundings to bfloat16 on the way count: a program that leaves them out, or rounds other values in their place, can miss the bound.
Values may be sent and summed in bfloat16 or wider, within the bound.
No kernel may reach another device: no remote copies, remote signals or barrier semaphores. Data moves between devices by JAX's collectives and lax.ppermute only.
A program may use at most 192 MiB of HBM per device.

```python
import jax
import jax.numpy as jnp
from jax import lax

D = 512
VARS = 227
GRID_DEV = 1024
EDGE_DEV = 4096
MESH_DEV = 320
CAP = 48
GRID = 32768
EDGES = 131072
MESH = 10240
BAND_NODES = 2560


def draw_edge_grid(key, part):
    devices = GRID // GRID_DEV
    local = jax.random.randint(jax.random.fold_in(key, 3), (devices, EDGE_DEV), 0, GRID_DEV)
    offset = jnp.arange(devices, dtype=jnp.int32)[:, None] * GRID_DEV
    return (local + offset).reshape(-1).astype(jnp.int32)


def draw_edge_mesh(key, part):
    devices = GRID // GRID_DEV
    owners = BAND_NODES // MESH_DEV
    bands = devices // owners
    keys = jax.random.split(jax.random.fold_in(key, 11), 4)
    band = jnp.arange(devices, dtype=jnp.int32) // owners
    middle = band == bands // 2
    upper = jnp.where(middle, CAP + 1, CAP * 3 // 4 + 1)
    counts = jax.random.randint(keys[0], (devices, owners), CAP // 2, upper[:, None])
    chosen = jax.random.randint(keys[1], (devices,), 0, owners)
    full = middle[:, None] & (jnp.arange(owners, dtype=jnp.int32)[None, :] == chosen[:, None])
    counts = jnp.where(full, CAP, counts)
    perm_keys = jax.random.split(keys[2], devices * owners)
    perms = jax.vmap(lambda k: jax.random.permutation(k, MESH_DEV))(perm_keys)
    perms = perms[:, :CAP].reshape(devices, owners, CAP).astype(jnp.int32)
    owner_base = jnp.arange(owners, dtype=jnp.int32)[None, :, None] * MESH_DEV
    candidates = (perms + owner_base).reshape(devices, owners * CAP)
    valid = (jnp.arange(CAP, dtype=jnp.int32)[None, None, :] < counts[:, :, None]).reshape(devices, owners * CAP)
    order = jnp.argsort(jnp.where(valid, 0, 1), axis=1, stable=True)
    touched = jnp.take_along_axis(candidates, order, axis=1)
    total = jnp.sum(counts, axis=1).astype(jnp.int32)
    picks = jax.random.randint(keys[3], (devices, EDGE_DEV), 0, 2 ** 30) % total[:, None]
    position = jnp.arange(EDGE_DEV, dtype=jnp.int32)[None, :]
    select = jnp.where(position < total[:, None], position, picks)
    nodes = jnp.sort(jnp.take_along_axis(touched, select, axis=1), axis=1)
    nodes = nodes + (band * BAND_NODES)[:, None]
    return nodes.reshape(-1).astype(jnp.int32)


def shard_levels(stream_key, shape, pieces, smallest, largest):
    def one(dim, shards_of):
        heights = jax.random.uniform(jax.random.fold_in(jax.random.fold_in(stream_key, 6), dim), (shards_of,), jnp.float32, smallest / len(pieces), largest / len(pieces))
        return jnp.repeat(jnp.exp(heights), shape[dim] // shards_of).reshape((-1,) + (1,) * (len(shape) - dim - 1))

    factor_of = one(*pieces[0])
    for cut in pieces[1:]:
        factor_of = factor_of * one(*cut)
    return factor_of


def noise(key, dims, scale, most, shards=(), kind=jnp.bfloat16):
    array = jax.random.normal(key, dims, jnp.float32) * scale
    if len(shards) > 0:
        array = shard_levels(key, dims, shards, -0.22, 0.18) * array
    return jnp.clip(array, min=-most, max=most).astype(kind)


def setup_inputs(seed: int = 0) -> dict:
    key_of = jax.random.split(jax.random.key(seed), 18)
    grid_vars = noise(key_of[0], (GRID, VARS), 1.0, 6.0, ((0, 32),))
    mesh_latent = noise(key_of[1], (MESH, D), 1.0, 6.0, ((0, 32),))
    cotangent = noise(key_of[2], (MESH, D), 1.0, 6.0, ((0, 32),))
    edge_grid = draw_edge_grid(jax.random.fold_in(key_of[17], 71), 0)
    edge_mesh = draw_edge_mesh(jax.random.fold_in(key_of[17], 71), 0)
    w_in = noise(key_of[5], (VARS, D), VARS ** -0.5, 0.375)
    b_in = noise(key_of[6], (D,), 1.0, 4.0, (), jnp.float32)
    w_out = noise(key_of[7], (D, D), D ** -0.5, 0.25)
    norm_gain = jnp.clip(1.0 + 0.18 * jax.random.normal(key_of[8], (D,), jnp.float32), 0.1, 1.9)
    u_grid = noise(key_of[9], (D, D), D ** -0.5, 0.25)
    u_mesh = noise(key_of[10], (D, D), D ** -0.5, 0.25)
    b_edge = noise(key_of[11], (D,), 1.0, 4.0, (), jnp.float32)
    w_edge = noise(key_of[12], (D, D), D ** -0.5, 0.25)
    w_self = noise(key_of[13], (D, D), D ** -0.5, 0.25)
    w_agg = noise(key_of[14], (D, D), (2 * D) ** -0.5, 0.1875)
    b_node = noise(key_of[15], (D,), 1.0, 4.0, (), jnp.float32)
    w_node_out = noise(key_of[16], (D, D), D ** -0.5, 0.25)
    return {"grid_vars": grid_vars, "mesh_latent": mesh_latent, "cotangent": cotangent, "edge_grid": edge_grid, "edge_mesh": edge_mesh, "w_in": w_in, "b_in": b_in, "w_out": w_out, "norm_gain": norm_gain, "u_grid": u_grid, "u_mesh": u_mesh, "b_edge": b_edge, "w_edge": w_edge, "w_self": w_self, "w_agg": w_agg, "b_node": b_node, "w_node_out": w_node_out}


def swish(v):
    return v * jax.nn.sigmoid(v)

def swish_grad(v):
    s = jax.nn.sigmoid(v)
    return s * (1.0 + v * (1.0 - s))

def layer_norm(v, gain):
    mean = lax.optimization_barrier(jnp.mean(v, axis=-1, keepdims=True))
    centred = v - mean
    var = lax.optimization_barrier(jnp.mean(centred * centred, axis=-1, keepdims=True))
    return centred * jax.lax.rsqrt(var + 1e-05) * gain

def mm(a, b):
    return jnp.dot(a, b, preferred_element_type=jnp.float32)

def reference(grid_vars, mesh_latent, cotangent, edge_grid, edge_mesh, w_in, b_in, w_out, norm_gain, u_grid, u_mesh, b_edge, w_edge, w_self, w_agg, b_node, w_node_out):
    hidden = swish(mm(grid_vars, w_in) + b_in).astype(jnp.bfloat16)
    latent = layer_norm(mm(hidden, w_out), norm_gain).astype(jnp.bfloat16)
    proj_grid = mm(latent, u_grid).astype(jnp.bfloat16)
    proj_mesh = mm(mesh_latent, u_mesh).astype(jnp.bfloat16)
    pre = proj_grid[edge_grid].astype(jnp.float32) + proj_mesh[edge_mesh].astype(jnp.float32) + b_edge
    act = swish(pre).astype(jnp.bfloat16)
    message = mm(act, w_edge).astype(jnp.bfloat16)
    agg = jax.ops.segment_sum(message.astype(jnp.float32), edge_mesh, num_segments=MESH).astype(jnp.bfloat16)
    node_pre = mm(mesh_latent, w_self) + mm(agg, w_agg) + b_node
    node_act = swish(node_pre).astype(jnp.bfloat16)
    mesh_out = (mesh_latent.astype(jnp.float32) + mm(node_act, w_node_out)).astype(jnp.bfloat16)
    g_node = (mm(cotangent, w_node_out.T) * swish_grad(node_pre)).astype(jnp.bfloat16)
    g_agg = mm(g_node, w_agg.T).astype(jnp.bfloat16)
    g_msg = g_agg[edge_mesh]
    scale = EDGES ** (-0.5)
    grad_edge = mm(act.T, g_msg) * scale
    g_edge = (mm(g_msg, w_edge.T) * swish_grad(pre)).astype(jnp.bfloat16)
    g_pgrid = jax.ops.segment_sum(g_edge.astype(jnp.float32), edge_grid, num_segments=GRID).astype(jnp.bfloat16)
    g_pmesh = jax.ops.segment_sum(g_edge.astype(jnp.float32), edge_mesh, num_segments=MESH).astype(jnp.bfloat16)
    grad_ugrid = mm(latent.T, g_pgrid) * scale
    grad_umesh = mm(mesh_latent.T, g_pmesh) * scale
    grad_mesh = (cotangent.astype(jnp.float32) + mm(g_node, w_self.T) + mm(g_pmesh, u_mesh.T)).astype(jnp.bfloat16)
    return (mesh_out, grad_mesh, grad_edge, grad_ugrid, grad_umesh)
```

```python
import functools

import jax
import jax.numpy as jnp
from jax import lax
from jax.experimental import pallas as pl
from jax.experimental.pallas import tpu as pltpu
from jax.sharding import Mesh
from jax.sharding import PartitionSpec as P

CAP = 48
LANES = 128
ROWS = 8
BF16 = jnp.bfloat16
F32 = jnp.float32


def dot(a, b):
    return jnp.dot(a, b, preferred_element_type=F32)


def dot_nt(a, b):
    return lax.dot_general(a, b, (((1,), (1,)), ((), ())), preferred_element_type=F32)


def dot_tn(a, b):
    return lax.dot_general(a, b, (((0,), (0,)), ((), ())), preferred_element_type=F32)


def sigmoid(v):
    return 0.5 + 0.5 * jnp.tanh(0.5 * v)


def as_bf16(mask):
    return jnp.where(mask, 1.0, 0.0).astype(BF16)


def edges_by_ids(ids, count):
    columns = jnp.transpose(ids)
    lanes = lax.broadcasted_iota(jnp.int32, (LANES, count), 1)
    return jnp.concatenate(
        [as_bf16(columns[:, j : j + 1] == lanes) for j in range(ids.shape[0])], axis=0
    )


def ids_by_edges(ids, count):
    places = lax.broadcasted_iota(jnp.int32, (count, LANES), 0)
    return jnp.concatenate(
        [as_bf16(ids[j : j + 1, :] == places) for j in range(ids.shape[0])], axis=1
    )


def call(kernel, name, out, args, flops, grid=None, in_specs=None, out_specs=None, scratch=(), vmem=24):
    moved = sum(a.size * a.dtype.itemsize for a in args)
    moved += sum(o.size * o.dtype.itemsize for o in out)
    extra = {}
    if grid is not None:
        extra = dict(grid=grid, in_specs=in_specs, out_specs=out_specs)
    return pl.pallas_call(
        kernel,
        out_shape=out,
        scratch_shapes=scratch,
        name=name,
        cost_estimate=pl.CostEstimate(flops=int(flops), bytes_accessed=int(moved), transcendentals=0),
        compiler_params=pltpu.CompilerParams(vmem_limit_bytes=vmem << 20),
        **extra,
    )(*args)


def whole(shape):
    return pl.BlockSpec(shape, lambda i: (0,) * len(shape))


def prep_kernel(owners, mesh_dev, em_ref, slot_ref, ids_ref):
    m = em_ref[...]
    rows = m.shape[0]
    lane = lax.broadcasted_iota(jnp.int32, m.shape, 1)
    row = lax.broadcasted_iota(jnp.int32, m.shape, 0)
    turned = pltpu.roll(m, 1, axis=1)
    before = jnp.where(lane == 0, pltpu.roll(turned, 1, axis=0), turned)
    fresh = (m != before) | ((lane == 0) & (row == 0))
    fresh_b = as_bf16(fresh)
    upto = lax.broadcasted_iota(jnp.int32, (LANES, LANES), 0) <= lax.broadcasted_iota(
        jnp.int32, (LANES, LANES), 1
    )
    inside = dot(fresh_b, as_bf16(upto))
    totals = jnp.broadcast_to(inside[:, LANES - 1 :], inside.shape).astype(BF16)
    above = lax.broadcasted_iota(jnp.int32, (rows, rows), 1) < lax.broadcasted_iota(
        jnp.int32, (rows, rows), 0
    )
    rank = (inside + dot(as_bf16(above), totals)).astype(jnp.int32) - 1
    slot = rank
    local = m
    fresh_i = fresh.astype(jnp.int32)
    for o in range(1, owners):
        past = m >= o * mesh_dev
        start = jnp.sum(
            jnp.sum(jnp.where(past, 0, fresh_i), axis=0, keepdims=True), axis=1, keepdims=True
        )
        slot = jnp.where(past, rank + (o * CAP - start), slot)
        local = jnp.where(past, m - o * mesh_dev, local)
    slot_ref[...] = slot
    value = jnp.where(fresh, local + 1, 0)
    found = []
    for o in range(owners):
        places = o * CAP + lax.broadcasted_iota(jnp.int32, (CAP, LANES), 0)
        total = jnp.zeros((CAP, LANES), jnp.int32)
        for r in range(rows):
            total = total + jnp.where(slot[r : r + 1, :] == places, value[r : r + 1, :], 0)
        found.append(total)
    pad = jnp.zeros((LANES - CAP, LANES), jnp.int32)
    for o in range(owners):
        square = jnp.transpose(jnp.concatenate([found[o], pad], axis=0))
        ids_ref[o : o + 1, :] = jnp.sum(square, axis=0, keepdims=True) - 1


def node_pre_kernel(ml_ref, cot_ref, um_ref, ws_ref, bn_ref, wno_ref, pm_ref, self_ref, cw_ref):
    ml = ml_ref[...]
    pm_ref[...] = dot(ml, um_ref[...]).astype(BF16)
    self_ref[...] = dot(ml, ws_ref[...]) + bn_ref[...]
    cw_ref[...] = dot_nt(cot_ref[...], wno_ref[...])


def embed_kernel(gv_ref, win_ref, bin_ref, wout_ref, gain_ref, ug_ref, lat_t_ref, pg_ref):
    v = dot(gv_ref[...], win_ref[...]) + bin_ref[...]
    hidden = (v * sigmoid(v)).astype(BF16)
    out = dot(hidden, wout_ref[...])
    mean = jnp.mean(out, axis=-1, keepdims=True)
    centred = out - mean
    var = jnp.mean(centred * centred, axis=-1, keepdims=True)
    latent = centred * lax.rsqrt(var + 1e-05) * gain_ref[...]
    pg_ref[...] = dot(latent.astype(BF16), ug_ref[...]).astype(BF16)
    lat_t_ref[...] = jnp.transpose(latent).astype(BF16)


def take_grid_kernel(ids_ref, pg_ref, out_ref):
    onehot = edges_by_ids(ids_ref[...], pg_ref.shape[0])
    out_ref[...] = dot(onehot, pg_ref[...]).astype(BF16)


def take_latent_kernel(ids_ref, lat_t_ref, out_ref):
    onehot = ids_by_edges(ids_ref[...], lat_t_ref.shape[1])
    out_ref[...] = dot(lat_t_ref[...], onehot).astype(BF16)


def ask_kernel(ids_ref, pm_ref, asked_ref, onehot_ref):
    owners = ids_ref.shape[0]
    nodes = pm_ref.shape[0]
    columns = jnp.transpose(ids_ref[...])
    lanes = lax.broadcasted_iota(jnp.int32, (CAP, nodes), 1)
    onehot = jnp.concatenate(
        [as_bf16(columns[:CAP, o : o + 1] == lanes) for o in range(owners)], axis=0
    )
    onehot_ref[...] = onehot
    asked_ref[...] = dot(onehot, pm_ref[...]).astype(BF16)


def pre_act(slot, pg, pm, bias):
    onehot = edges_by_ids(slot, pm.shape[0])
    return dot(onehot, pm) + pg.astype(F32) + bias


def edge_kernel(steps, slot_ref, pg_ref, pm_ref, be_ref, sum_ref, total):
    step = pl.program_id(0)

    @pl.when(step == 0)
    def _():
        total[...] = jnp.zeros_like(total)

    slot = slot_ref[...]
    pre = pre_act(slot, pg_ref[...], pm_ref[...], be_ref[...])
    act = (pre * sigmoid(pre)).astype(BF16)
    total[...] += dot(ids_by_edges(slot, total.shape[0]), act)

    @pl.when(step == steps - 1)
    def _():
        sum_ref[...] = total[...].astype(BF16)


def slope_kernel(steps, slot_ref, pg_ref, pm_ref, be_ref, slope_ref, sum_ref, total):
    step = pl.program_id(0)

    @pl.when(step == 0)
    def _():
        total[...] = jnp.zeros_like(total)

    slot = slot_ref[...]
    pre = pre_act(slot, pg_ref[...], pm_ref[...], be_ref[...])
    s = sigmoid(pre)
    slope = s * (1.0 + pre * (1.0 - s))
    slope_ref[...] = slope
    total[...] += dot(ids_by_edges(slot, total.shape[0]), slope.astype(BF16))

    @pl.when(step == steps - 1)
    def _():
        sum_ref[...] = total[...].astype(BF16)


def node_kernel(
    rec_ref, row_ref, oh_ref, self_ref, cw_ref, we_ref, wa_ref,
    hask_ref, act_ref, h_ref, gagg_ref, gnode_ref, nact_ref,
):
    nodes = self_ref.shape[0]
    onehot_t = as_bf16(lax.broadcasted_iota(jnp.int32, (nodes, row_ref.shape[1]), 0) == row_ref[...])
    act = dot(onehot_t, rec_ref[...]).astype(BF16)
    agg = dot(act, we_ref[...]).astype(BF16)
    pre = self_ref[...] + dot(agg, wa_ref[...])
    s = sigmoid(pre)
    g_node = (cw_ref[...] * (s * (1.0 + pre * (1.0 - s)))).astype(BF16)
    g_agg = dot_nt(g_node, wa_ref[...]).astype(BF16)
    h = dot_nt(g_agg, we_ref[...])
    hask_ref[...] = dot(oh_ref[...], h.astype(BF16)).astype(BF16)
    act_ref[...] = act
    h_ref[...] = h
    gagg_ref[...] = g_agg
    gnode_ref[...] = g_node
    nact_ref[...] = (pre * s).astype(BF16)


def node_post_kernel(
    rec_ref, row_ref, act_ref, h_ref, gagg_ref, gnode_ref, nact_ref, ml_ref, cot_ref,
    wno_ref, ws_ref, um_ref, mo_ref, gm_ref, grads_ref,
):
    nodes, width = h_ref.shape
    ml = ml_ref[...]
    onehot_t = as_bf16(lax.broadcasted_iota(jnp.int32, (nodes, row_ref.shape[1]), 0) == row_ref[...])
    slopes = dot(onehot_t, rec_ref[...])
    g_pmesh = (h_ref[...] * slopes).astype(BF16)
    grads_ref[:width, :] = dot_tn(act_ref[...], gagg_ref[...]).astype(BF16)
    grads_ref[width:, :] = dot_tn(ml, g_pmesh).astype(BF16)
    mo_ref[...] = (ml.astype(F32) + dot(nact_ref[...], wno_ref[...])).astype(BF16)
    gm_ref[...] = (
        cot_ref[...].astype(F32) + dot_nt(gnode_ref[...], ws_ref[...]) + dot_nt(g_pmesh, um_ref[...])
    ).astype(BF16)


def edge_back_kernel(steps, slot_ref, slope_ref, lat_t_ref, h_ref, out_ref, total):
    step = pl.program_id(0)

    @pl.when(step == 0)
    def _():
        total[...] = jnp.zeros_like(total)

    onehot = edges_by_ids(slot_ref[...], h_ref.shape[0])
    g_edge = (dot(onehot, h_ref[...]) * slope_ref[...]).astype(BF16)
    total[...] += dot(lat_t_ref[...], g_edge)

    @pl.when(step == steps - 1)
    def _():
        out_ref[...] = total[...].astype(BF16)


def all_sum(value, scale):
    rows, width = value.shape
    half = rows // 2
    core = lax.axis_index("core")
    pairs = [(0, 1), (1, 0)]
    others = ("x", "mesh")
    count = lax.axis_size("x") * lax.axis_size("mesh")
    keep = lax.dynamic_slice_in_dim(value, core * half, half, 0)
    give = lax.dynamic_slice_in_dim(value, (1 - core) * half, half, 0)
    got = lax.ppermute(give, "core", pairs)
    part = (keep.astype(F32) + got.astype(F32)).astype(BF16)
    pieces = lax.all_to_all(part, others, 0, 0, tiled=True).reshape(count, half // count, width)
    total = (jnp.sum(pieces.astype(F32), axis=0) * scale).astype(BF16)
    copies = jnp.broadcast_to(total[None], pieces.shape).reshape(half, width)
    mine = lax.all_to_all(copies, others, 0, 0, tiled=True)
    other = lax.ppermute(mine, "core", pairs)
    first = jnp.where(core == 0, mine, other)
    second = jnp.where(core == 0, other, mine)
    return jnp.concatenate([first, second], axis=0).astype(F32)


def shards(
    grid_vars,
    mesh_latent,
    cotangent,
    edge_grid,
    edge_mesh,
    w_in,
    b_in,
    w_out,
    norm_gain,
    u_grid,
    u_mesh,
    b_edge,
    w_edge,
    w_self,
    w_agg,
    b_node,
    w_node_out,
):
    grid_dev, variables = grid_vars.shape
    mesh_dev, width = mesh_latent.shape
    edge_dev = edge_grid.shape[0]
    owners = lax.axis_size("mesh")
    slots = owners * CAP
    rows = edge_dev // LANES
    block = ROWS * LANES
    steps = edge_dev // block
    band = lax.axis_index("x") * lax.axis_size("core") + lax.axis_index("core")
    device = band * owners + lax.axis_index("mesh")
    scale = (edge_dev * lax.axis_size("x") * lax.axis_size("core") * owners) ** (-0.5)
    sds = jax.ShapeDtypeStruct

    def exchange(value):
        return lax.all_to_all(value, "mesh", 0, 0, tiled=True)

    mesh_local = (edge_mesh - band * (owners * mesh_dev)).reshape(rows, LANES)
    grid_local = (edge_grid - device * grid_dev).reshape(rows, LANES)

    slot, ids = call(
        functools.partial(prep_kernel, owners, mesh_dev),
        "prep",
        [sds((rows, LANES), jnp.int32), sds((owners, LANES), jnp.int32)],
        [mesh_local],
        1e9,
    )
    incoming = exchange(ids)

    proj_mesh, self_part, cot_part = call(
        node_pre_kernel,
        "node_pre",
        [sds((mesh_dev, width), BF16), sds((mesh_dev, width), F32), sds((mesh_dev, width), F32)],
        [mesh_latent, cotangent, u_mesh, w_self, b_node.reshape(1, width), w_node_out],
        6 * mesh_dev * width * width,
    )

    tile = min(256, grid_dev)
    latent_t, proj_grid = call(
        embed_kernel,
        "embed",
        [sds((width, grid_dev), BF16), sds((grid_dev, width), BF16)],
        [grid_vars, w_in, b_in.reshape(1, width), w_out, norm_gain.reshape(1, width), u_grid],
        2 * grid_dev * width * (variables + 2 * width),
        grid=(grid_dev // tile,),
        in_specs=[
            pl.BlockSpec((tile, variables), lambda i: (i, 0)),
            whole((variables, width)),
            whole((1, width)),
            whole((width, width)),
            whole((1, width)),
            whole((width, width)),
        ],
        out_specs=[
            pl.BlockSpec((width, tile), lambda i: (0, i)),
            pl.BlockSpec((tile, width), lambda i: (i, 0)),
        ],
    )

    id_spec = pl.BlockSpec((ROWS, LANES), lambda i: (i, 0))
    edge_spec = pl.BlockSpec((block, width), lambda i: (i, 0))
    edge_t_spec = pl.BlockSpec((width, block), lambda i: (0, i))
    (edge_pgrid,) = call(
        take_grid_kernel,
        "take_grid",
        [sds((edge_dev, width), BF16)],
        [grid_local, proj_grid],
        2 * edge_dev * grid_dev * width,
        grid=(steps,),
        in_specs=[id_spec, whole((grid_dev, width))],
        out_specs=[edge_spec],
    )
    (edge_latent_t,) = call(
        take_latent_kernel,
        "take_latent",
        [sds((width, edge_dev), BF16)],
        [grid_local, latent_t],
        2 * edge_dev * grid_dev * width,
        grid=(steps,),
        in_specs=[id_spec, whole((width, grid_dev))],
        out_specs=[edge_t_spec],
    )

    asked, onehot_in = call(
        ask_kernel,
        "ask",
        [sds((slots, width), BF16), sds((slots, mesh_dev), BF16)],
        [incoming, proj_mesh],
        2 * slots * mesh_dev * width,
    )
    incoming_row = incoming[:, :CAP].reshape(1, slots)
    slot_pmesh = exchange(asked)

    bias = b_edge.reshape(1, width)
    forward_specs = [id_spec, edge_spec, whole((slots, width)), whole((1, width))]
    total = [pltpu.VMEM((slots, width), F32)]
    (act_sums,) = call(
        functools.partial(edge_kernel, steps),
        "edge",
        [sds((slots, width), BF16)],
        [slot, edge_pgrid, slot_pmesh, bias],
        4 * edge_dev * slots * width,
        grid=(steps,),
        in_specs=forward_specs,
        out_specs=[whole((slots, width))],
        scratch=total,
    )
    act_received = exchange(act_sums)
    slope, slope_sums = call(
        functools.partial(slope_kernel, steps),
        "slope",
        [sds((edge_dev, width), F32), sds((slots, width), BF16)],
        [slot, edge_pgrid, slot_pmesh, bias],
        4 * edge_dev * slots * width,
        grid=(steps,),
        in_specs=forward_specs,
        out_specs=[edge_spec, whole((slots, width))],
        scratch=total,
    )
    slope_received = exchange(slope_sums)

    node_b = sds((mesh_dev, width), BF16)
    h_asked, act_total, h, g_agg, g_node, node_act = call(
        node_kernel,
        "node",
        [sds((slots, width), BF16), node_b, sds((mesh_dev, width), F32), node_b, node_b, node_b],
        [act_received, incoming_row, onehot_in, self_part, cot_part, w_edge, w_agg],
        8 * mesh_dev * width * width + 4 * mesh_dev * slots * width,
    )
    slot_h = exchange(h_asked)

    mesh_out, grad_mesh, owner_grads = call(
        node_post_kernel,
        "node_post",
        [node_b, node_b, sds((2 * width, width), BF16)],
        [
            slope_received, incoming_row, act_total, h, g_agg, g_node, node_act,
            mesh_latent, cotangent, w_node_out, w_self, u_mesh,
        ],
        10 * mesh_dev * width * width + 2 * mesh_dev * slots * width,
    )
    owner_total = all_sum(owner_grads, scale)

    (local_ugrid,) = call(
        functools.partial(edge_back_kernel, steps),
        "edge_back",
        [sds((width, width), BF16)],
        [slot, slope, edge_latent_t, slot_h],
        2 * edge_dev * (slots + width) * width,
        grid=(steps,),
        in_specs=[id_spec, edge_spec, edge_t_spec, whole((slots, width))],
        out_specs=[whole((width, width))],
        scratch=[pltpu.VMEM((width, width), F32)],
    )
    grad_ugrid = all_sum(local_ugrid, scale)
    return mesh_out, grad_mesh, owner_total[:width], grad_ugrid, owner_total[width:]


def solution(mesh):
    bands, owners = mesh.shape["band"], mesh.shape["mesh"]
    cores = 2
    fine = Mesh(mesh.devices.reshape(bands // cores, cores, owners), ("x", "core", "mesh"))
    split = ("x", "core", "mesh")
    return jax.shard_map(
        shards,
        mesh=fine,
        in_specs=(P(split, None),) * 3 + (P(split),) * 2 + (P(),) * 12,
        out_specs=(P(split, None), P(split, None), P(), P(), P()),
        check_vma=False,
    )
```

```python
import functools

import jax
import jax.numpy as jnp
from jax import lax
from jax.experimental import pallas as pl
from jax.experimental.pallas import tpu as pltpu
from jax.sharding import Mesh
from jax.sharding import PartitionSpec as P

CAP = 48
LANES = 128
ROWS = 8
BF16 = jnp.bfloat16
F32 = jnp.float32


def dot(a, b):
    return jnp.dot(a, b, preferred_element_type=F32)


def dot_nt(a, b):
    return lax.dot_general(a, b, (((1,), (1,)), ((), ())), preferred_element_type=F32)


def dot_tn(a, b):
    return lax.dot_general(a, b, (((0,), (0,)), ((), ())), preferred_element_type=F32)


def sigmoid(v):
    return 0.5 + 0.5 * jnp.tanh(0.5 * v)


def as_bf16(mask):
    return jnp.where(mask, 1.0, 0.0).astype(BF16)


def edges_by_ids(ids, count):
    columns = jnp.transpose(ids)
    lanes = lax.broadcasted_iota(jnp.int32, (LANES, count), 1)
    return jnp.concatenate(
        [as_bf16(columns[:, j : j + 1] == lanes) for j in range(ids.shape[0])], axis=0
    )


def ids_by_edges(ids, count):
    places = lax.broadcasted_iota(jnp.int32, (count, LANES), 0)
    return jnp.concatenate(
        [as_bf16(ids[j : j + 1, :] == places) for j in range(ids.shape[0])], axis=1
    )


def call(kernel, name, out, args, flops, grid=None, in_specs=None, out_specs=None, scratch=(), vmem=60):
    moved = sum(a.size * a.dtype.itemsize for a in args)
    moved += sum(o.size * o.dtype.itemsize for o in out)
    extra = {}
    if grid is not None:
        extra = dict(grid=grid, in_specs=in_specs, out_specs=out_specs)
    return pl.pallas_call(
        kernel,
        out_shape=out,
        scratch_shapes=scratch,
        name=name,
        cost_estimate=pl.CostEstimate(flops=int(flops), bytes_accessed=int(moved), transcendentals=0),
        compiler_params=pltpu.CompilerParams(vmem_limit_bytes=vmem << 20),
        **extra,
    )(*args)


def whole(shape):
    return pl.BlockSpec(shape, lambda i: (0,) * len(shape))


def prep_kernel(owners, mesh_dev, em_ref, slot_ref, ids_ref):
    m = em_ref[...]
    rows = m.shape[0]
    lane = lax.broadcasted_iota(jnp.int32, m.shape, 1)
    row = lax.broadcasted_iota(jnp.int32, m.shape, 0)
    turned = pltpu.roll(m, 1, axis=1)
    before = jnp.where(lane == 0, pltpu.roll(turned, 1, axis=0), turned)
    fresh = (m != before) | ((lane == 0) & (row == 0))
    fresh_b = as_bf16(fresh)
    upto = lax.broadcasted_iota(jnp.int32, (LANES, LANES), 0) <= lax.broadcasted_iota(
        jnp.int32, (LANES, LANES), 1
    )
    inside = dot(fresh_b, as_bf16(upto))
    totals = jnp.broadcast_to(inside[:, LANES - 1 :], inside.shape).astype(BF16)
    above = lax.broadcasted_iota(jnp.int32, (rows, rows), 1) < lax.broadcasted_iota(
        jnp.int32, (rows, rows), 0
    )
    rank = (inside + dot(as_bf16(above), totals)).astype(jnp.int32) - 1
    slot = rank
    local = m
    fresh_i = fresh.astype(jnp.int32)
    for o in range(1, owners):
        past = m >= o * mesh_dev
        start = jnp.sum(
            jnp.sum(jnp.where(past, 0, fresh_i), axis=0, keepdims=True), axis=1, keepdims=True
        )
        slot = jnp.where(past, rank + (o * CAP - start), slot)
        local = jnp.where(past, m - o * mesh_dev, local)
    slot_ref[...] = slot
    value = jnp.where(fresh, local + 1, 0)
    found = []
    for o in range(owners):
        places = o * CAP + lax.broadcasted_iota(jnp.int32, (CAP, LANES), 0)
        total = jnp.zeros((CAP, LANES), jnp.int32)
        for r in range(rows):
            total = total + jnp.where(slot[r : r + 1, :] == places, value[r : r + 1, :], 0)
        found.append(total)
    pad = jnp.zeros((LANES - CAP, LANES), jnp.int32)
    for o in range(owners):
        square = jnp.transpose(jnp.concatenate([found[o], pad], axis=0))
        ids_ref[o : o + 1, :] = jnp.sum(square, axis=0, keepdims=True) - 1


def node_pre_kernel(ml_ref, cot_ref, um_ref, ws_ref, bn_ref, wno_ref, pm_ref, self_ref, cw_ref):
    ml = ml_ref[...]
    pm_ref[...] = dot(ml, um_ref[...]).astype(BF16)
    self_ref[...] = dot(ml, ws_ref[...]) + bn_ref[...]
    cw_ref[...] = dot_nt(cot_ref[...], wno_ref[...])


def embed_kernel(gv_ref, win_ref, bin_ref, wout_ref, gain_ref, ug_ref, lat_t_ref, pg_ref):
    v = dot(gv_ref[...], win_ref[...]) + bin_ref[...]
    hidden = (v * sigmoid(v)).astype(BF16)
    out = dot(hidden, wout_ref[...])
    mean = jnp.mean(out, axis=-1, keepdims=True)
    centred = out - mean
    var = jnp.mean(centred * centred, axis=-1, keepdims=True)
    latent = centred * lax.rsqrt(var + 1e-05) * gain_ref[...]
    pg_ref[...] = dot(latent.astype(BF16), ug_ref[...]).astype(BF16)
    lat_t_ref[...] = jnp.transpose(latent).astype(BF16)


def take_grid_kernel(ids_ref, pg_ref, out_ref):
    onehot = edges_by_ids(ids_ref[...], pg_ref.shape[0])
    out_ref[...] = dot(onehot, pg_ref[...]).astype(BF16)


def take_latent_kernel(ids_ref, lat_t_ref, out_ref):
    onehot = ids_by_edges(ids_ref[...], lat_t_ref.shape[1])
    out_ref[...] = dot(lat_t_ref[...], onehot).astype(BF16)


def ask_kernel(ids_ref, pm_ref, asked_ref, onehot_ref):
    owners = ids_ref.shape[0]
    nodes = pm_ref.shape[0]
    columns = jnp.transpose(ids_ref[...])
    lanes = lax.broadcasted_iota(jnp.int32, (CAP, nodes), 1)
    onehot = jnp.concatenate(
        [as_bf16(columns[:CAP, o : o + 1] == lanes) for o in range(owners)], axis=0
    )
    onehot_ref[...] = onehot
    asked_ref[...] = dot(onehot, pm_ref[...]).astype(BF16)


def edge_kernel(steps, slot_ref, pg_ref, pm_ref, be_ref, we_ref, slope_ref, sums_ref, act_ref, acts, slopes):
    step = pl.program_id(0)

    @pl.when(step == 0)
    def _():
        acts[...] = jnp.zeros_like(acts)
        slopes[...] = jnp.zeros_like(slopes)

    slot = slot_ref[...]
    slots, width = acts.shape
    pre = dot(edges_by_ids(slot, slots), pm_ref[...]) + pg_ref[...].astype(F32) + be_ref[...]
    s = sigmoid(pre)
    act = pre * s
    slope = s * (1.0 + pre - act)
    slope_ref[...] = slope
    onehot_t = ids_by_edges(slot, slots)
    acts[...] += dot(onehot_t, act.astype(BF16))
    slopes[...] += dot(onehot_t, slope.astype(BF16))

    @pl.when(step == steps - 1)
    def _():
        total = acts[...]
        high = total.astype(BF16)
        low = (total - high.astype(F32)).astype(BF16)
        act_ref[...] = high
        sums_ref[:, :width] = (dot(high, we_ref[...]) + dot(low, we_ref[...])).astype(BF16)
        sums_ref[:, width:] = slopes[...].astype(BF16)


def node_kernel(rec_ref, row_ref, oh_ref, self_ref, cw_ref, wa_ref, gask_ref, gagg_ref, gnode_ref, nact_ref):
    nodes, width = self_ref.shape
    onehot_t = as_bf16(lax.broadcasted_iota(jnp.int32, (nodes, row_ref.shape[1]), 0) == row_ref[...])
    agg = dot(onehot_t, rec_ref[:, :width]).astype(BF16)
    pre = self_ref[...] + dot(agg, wa_ref[...])
    s = sigmoid(pre)
    act = pre * s
    g_node = (cw_ref[...] * (s * (1.0 + pre - act))).astype(BF16)
    g_agg = dot_nt(g_node, wa_ref[...]).astype(BF16)
    gask_ref[...] = dot(oh_ref[...], g_agg).astype(BF16)
    gagg_ref[...] = g_agg
    gnode_ref[...] = g_node
    nact_ref[...] = act.astype(BF16)


def node_post_kernel(
    rec_ref, row_ref, gagg_ref, gnode_ref, nact_ref, ml_ref, cot_ref,
    we_ref, wno_ref, ws_ref, um_ref, mo_ref, gm_ref, keep_ref, give_ref,
):
    nodes, width = gagg_ref.shape
    half = width // 2
    ml = ml_ref[...]
    onehot_t = as_bf16(lax.broadcasted_iota(jnp.int32, (nodes, row_ref.shape[1]), 0) == row_ref[...])
    slopes = dot(onehot_t, rec_ref[:, width:])
    g_pmesh = (dot_nt(gagg_ref[...], we_ref[...]) * slopes).astype(BF16)
    grad = dot_tn(ml, g_pmesh).astype(BF16)
    put_halves(grad[:half], grad[half:], keep_ref, give_ref)
    mo_ref[...] = (ml.astype(F32) + dot(nact_ref[...], wno_ref[...])).astype(BF16)
    gm_ref[...] = (
        cot_ref[...].astype(F32) + dot_nt(gnode_ref[...], ws_ref[...]) + dot_nt(g_pmesh, um_ref[...])
    ).astype(BF16)


def put_halves(first, second, keep_ref, give_ref):
    core = lax.axis_index("core")

    @pl.when(core == 0)
    def _():
        keep_ref[...] = first
        give_ref[...] = second

    @pl.when(core != 0)
    def _():
        keep_ref[...] = second
        give_ref[...] = first


def edge_back_kernel(
    steps, slot_ref, slope_ref, lat_t_ref, gc_ref, act_ref, we_ref, keep_ref, give_ref, total, h
):
    step = pl.program_id(0)

    @pl.when(step == 0)
    def _():
        total[...] = jnp.zeros_like(total)
        h[...] = dot_nt(gc_ref[...], we_ref[...]).astype(BF16)

    onehot = edges_by_ids(slot_ref[...], h.shape[0])
    g_edge = (dot(onehot, h[...]) * slope_ref[...]).astype(BF16)
    total[...] += dot(lat_t_ref[...], g_edge)

    @pl.when(step == steps - 1)
    def _():
        grad_edge = dot_tn(act_ref[...], gc_ref[...]).astype(BF16)
        put_halves(total[...].astype(BF16), grad_edge, keep_ref, give_ref)


def add_kernel(keep_ref, got_ref, out_ref):
    out_ref[...] = (keep_ref[...].astype(F32) + got_ref[...].astype(F32)).astype(BF16)


def spread_kernel(scale, umesh_ref, pair_ref, out_ref):
    low, high = umesh_ref.shape[1], pair_ref.shape[1]
    umesh = jnp.sum(umesh_ref[...].astype(F32), axis=0) * scale
    pair = jnp.sum(pair_ref[...].astype(F32), axis=0) * scale
    total = jnp.concatenate([umesh, pair], axis=0).astype(BF16)
    out_ref[...] = jnp.broadcast_to(total[None], out_ref.shape)


def finish_kernel(mine_ref, other_ref, edge_ref, ugrid_ref, umesh_ref):
    count, _, width = mine_ref.shape
    low = umesh_ref.shape[0] // 2 // count
    core = lax.axis_index("core")

    def put(first_ref, second_ref):
        half = count * low
        umesh_ref[:half] = first_ref[:, :low].astype(F32).reshape(half, width)
        umesh_ref[half:] = second_ref[:, :low].astype(F32).reshape(half, width)
        ugrid_ref[...] = first_ref[:, low:].astype(F32).reshape(2 * half, width)
        edge_ref[...] = second_ref[:, low:].astype(F32).reshape(2 * half, width)

    @pl.when(core == 0)
    def _():
        put(mine_ref, other_ref)

    @pl.when(core != 0)
    def _():
        put(other_ref, mine_ref)


def pair_sum(keep, give, name):
    got = lax.ppermute(give, "core", [(0, 1), (1, 0)])
    (out,) = call(add_kernel, name, [jax.ShapeDtypeStruct(keep.shape, BF16)], [keep, got], keep.size)
    return out


def shards(
    grid_vars,
    mesh_latent,
    cotangent,
    edge_grid,
    edge_mesh,
    w_in,
    b_in,
    w_out,
    norm_gain,
    u_grid,
    u_mesh,
    b_edge,
    w_edge,
    w_self,
    w_agg,
    b_node,
    w_node_out,
):
    grid_dev, variables = grid_vars.shape
    mesh_dev, width = mesh_latent.shape
    edge_dev = edge_grid.shape[0]
    owners = lax.axis_size("mesh")
    slots = owners * CAP
    rows = edge_dev // LANES
    block = ROWS * LANES
    steps = edge_dev // block
    band = lax.axis_index("x") * lax.axis_size("core") + lax.axis_index("core")
    device = band * owners + lax.axis_index("mesh")
    scale = (edge_dev * lax.axis_size("x") * lax.axis_size("core") * owners) ** (-0.5)
    sds = jax.ShapeDtypeStruct

    def exchange(value):
        return lax.all_to_all(value, "mesh", 0, 0, tiled=True)

    mesh_local = (edge_mesh - band * (owners * mesh_dev)).reshape(rows, LANES)
    grid_local = (edge_grid - device * grid_dev).reshape(rows, LANES)

    slot, ids = call(
        functools.partial(prep_kernel, owners, mesh_dev),
        "prep",
        [sds((rows, LANES), jnp.int32), sds((owners, LANES), jnp.int32)],
        [mesh_local],
        1e9,
    )
    incoming = exchange(ids)

    proj_mesh, self_part, cot_part = call(
        node_pre_kernel,
        "node_pre",
        [sds((mesh_dev, width), BF16), sds((mesh_dev, width), F32), sds((mesh_dev, width), F32)],
        [mesh_latent, cotangent, u_mesh, w_self, b_node.reshape(1, width), w_node_out],
        6 * mesh_dev * width * width,
    )

    tile = min(256, grid_dev)
    latent_t, proj_grid = call(
        embed_kernel,
        "embed",
        [sds((width, grid_dev), BF16), sds((grid_dev, width), BF16)],
        [grid_vars, w_in, b_in.reshape(1, width), w_out, norm_gain.reshape(1, width), u_grid],
        2 * grid_dev * width * (variables + 2 * width),
        grid=(grid_dev // tile,),
        in_specs=[
            pl.BlockSpec((tile, variables), lambda i: (i, 0)),
            whole((variables, width)),
            whole((1, width)),
            whole((width, width)),
            whole((1, width)),
            whole((width, width)),
        ],
        out_specs=[
            pl.BlockSpec((width, tile), lambda i: (0, i)),
            pl.BlockSpec((tile, width), lambda i: (i, 0)),
        ],
    )

    id_spec = pl.BlockSpec((ROWS, LANES), lambda i: (i, 0))
    edge_spec = pl.BlockSpec((block, width), lambda i: (i, 0))
    edge_t_spec = pl.BlockSpec((width, block), lambda i: (0, i))
    (edge_pgrid,) = call(
        take_grid_kernel,
        "take_grid",
        [sds((edge_dev, width), BF16)],
        [grid_local, proj_grid],
        2 * edge_dev * grid_dev * width,
        grid=(steps,),
        in_specs=[id_spec, whole((grid_dev, width))],
        out_specs=[edge_spec],
    )
    (edge_latent_t,) = call(
        take_latent_kernel,
        "take_latent",
        [sds((width, edge_dev), BF16)],
        [grid_local, latent_t],
        2 * edge_dev * grid_dev * width,
        grid=(steps,),
        in_specs=[id_spec, whole((width, grid_dev))],
        out_specs=[edge_t_spec],
    )

    asked, onehot_in = call(
        ask_kernel,
        "ask",
        [sds((slots, width), BF16), sds((slots, mesh_dev), BF16)],
        [incoming, proj_mesh],
        2 * slots * mesh_dev * width,
    )
    incoming_row = incoming[:, :CAP].reshape(1, slots)
    slot_pmesh = exchange(asked)

    sums_b = sds((slots, width), BF16)
    slope, sums, act_sums = call(
        functools.partial(edge_kernel, steps),
        "edge",
        [sds((edge_dev, width), F32), sds((slots, 2 * width), BF16), sums_b],
        [slot, edge_pgrid, slot_pmesh, b_edge.reshape(1, width), w_edge],
        6 * edge_dev * slots * width,
        grid=(steps,),
        in_specs=[id_spec, edge_spec, whole((slots, width)), whole((1, width)), whole((width, width))],
        out_specs=[edge_spec, whole((slots, 2 * width)), whole((slots, width))],
        scratch=[pltpu.VMEM((slots, width), F32), pltpu.VMEM((slots, width), F32)],
    )
    received = exchange(sums)

    node_b = sds((mesh_dev, width), BF16)
    g_asked, g_agg, g_node, node_act = call(
        node_kernel,
        "node",
        [sums_b, node_b, node_b, node_b],
        [received, incoming_row, onehot_in, self_part, cot_part, w_agg],
        4 * mesh_dev * width * width + 4 * mesh_dev * slots * width,
    )
    slot_g = exchange(g_asked)

    half = sds((width // 2, width), BF16)
    mesh_out, grad_mesh, keep, give = call(
        node_post_kernel,
        "node_post",
        [node_b, node_b, half, half],
        [
            received, incoming_row, g_agg, g_node, node_act, mesh_latent, cotangent,
            w_edge, w_node_out, w_self, u_mesh,
        ],
        10 * mesh_dev * width * width + 2 * mesh_dev * slots * width,
    )
    others = ("x", "mesh")
    count = lax.axis_size("x") * owners
    umesh_parts = lax.all_to_all(pair_sum(keep, give, "add_umesh"), others, 0, 0, tiled=True)

    full = sds((width, width), BF16)
    keep, give = call(
        functools.partial(edge_back_kernel, steps),
        "edge_back",
        [full, full],
        [slot, slope, edge_latent_t, slot_g, act_sums, w_edge],
        2 * edge_dev * (slots + width) * width,
        grid=(steps,),
        in_specs=[
            id_spec, edge_spec, edge_t_spec, whole((slots, width)), whole((slots, width)),
            whole((width, width)),
        ],
        out_specs=[whole((width, width)), whole((width, width))],
        scratch=[pltpu.VMEM((width, width), F32), pltpu.VMEM((slots, width), BF16)],
    )
    pair_parts = lax.all_to_all(pair_sum(keep, give, "add_pair"), others, 0, 0, tiled=True)

    low = width // 2 // count
    (copies,) = call(
        functools.partial(spread_kernel, scale),
        "spread",
        [sds((count, 3 * low, width), BF16)],
        [umesh_parts.reshape(count, low, width), pair_parts.reshape(count, 2 * low, width)],
        3 * count * low * width,
    )
    mine = lax.all_to_all(copies, others, 0, 0, tiled=True)
    other = lax.ppermute(mine, "core", [(0, 1), (1, 0)])
    weight = sds((width, width), F32)
    grad_edge, grad_ugrid, grad_umesh = call(
        finish_kernel, "finish", [weight, weight, weight], [mine, other], 3 * width * width
    )
    return mesh_out, grad_mesh, grad_edge, grad_ugrid, grad_umesh


def solution(mesh):
    bands, owners = mesh.shape["band"], mesh.shape["mesh"]
    cores = 2
    fine = Mesh(mesh.devices.reshape(bands // cores, cores, owners), ("x", "core", "mesh"))
    split = ("x", "core", "mesh")
    return jax.shard_map(
        shards,
        mesh=fine,
        in_specs=(P(split, None),) * 3 + (P(split),) * 2 + (P(),) * 12,
        out_specs=(P(split, None), P(split, None), P(), P(), P()),
        check_vma=False,
    )
```

```python
import functools

import jax
import jax.numpy as jnp
from jax import lax
from jax.experimental import pallas as pl
from jax.experimental.pallas import tpu as pltpu
from jax.sharding import Mesh
from jax.sharding import PartitionSpec as P

CAP = 48
LANES = 128
ROWS = 8
BF16 = jnp.bfloat16
F32 = jnp.float32


def dot(a, b):
    return jnp.dot(a, b, preferred_element_type=F32)


def dot_nt(a, b):
    return lax.dot_general(a, b, (((1,), (1,)), ((), ())), preferred_element_type=F32)


def dot_tn(a, b):
    return lax.dot_general(a, b, (((0,), (0,)), ((), ())), preferred_element_type=F32)


def sigmoid(v):
    return 0.5 + 0.5 * jnp.tanh(0.5 * v)


def as_bf16(mask):
    return jnp.where(mask, 1.0, 0.0).astype(BF16)


def edges_by_ids(ids, count):
    columns = jnp.transpose(ids)
    lanes = lax.broadcasted_iota(jnp.int32, (LANES, count), 1)
    return jnp.concatenate(
        [as_bf16(columns[:, j : j + 1] == lanes) for j in range(ids.shape[0])], axis=0
    )


def ids_by_edges(ids, count):
    places = lax.broadcasted_iota(jnp.int32, (count, LANES), 0)
    return jnp.concatenate(
        [as_bf16(ids[j : j + 1, :] == places) for j in range(ids.shape[0])], axis=1
    )


def call(kernel, name, out, args, flops, grid=None, in_specs=None, out_specs=None, scratch=(), vmem=16, after=()):
    moved = sum(a.size * a.dtype.itemsize for a in args)
    moved += sum(o.size * o.dtype.itemsize for o in out)
    count = len(args)

    def body(*refs):
        kernel(*refs[:count], *refs[count + len(after) :])

    if in_specs is None:
        in_specs = [pl.BlockSpec(memory_space=pltpu.VMEM)] * count
    extra = {} if grid is None else dict(grid=grid)
    if out_specs is not None:
        extra["out_specs"] = out_specs
    return pl.pallas_call(
        body,
        out_shape=out,
        in_specs=list(in_specs) + [pl.BlockSpec(memory_space=pl.ANY)] * len(after),
        scratch_shapes=scratch,
        name=name,
        cost_estimate=pl.CostEstimate(flops=int(flops), bytes_accessed=int(moved), transcendentals=0),
        compiler_params=pltpu.CompilerParams(vmem_limit_bytes=vmem << 20),
        **extra,
    )(*args, *after)


def whole(shape):
    return pl.BlockSpec(shape, lambda i: (0,) * len(shape))


def band_index():
    return lax.axis_index("x") * lax.axis_size("core") + lax.axis_index("core")


def grid_block(ids_ref, count):
    device = band_index() * lax.axis_size("mesh") + lax.axis_index("mesh")
    return ids_ref[...] - device * count


def prep_kernel(owners, mesh_dev, em_ref, slot_ref, ids_ref):
    m = em_ref[...] - band_index() * (owners * mesh_dev)
    rows = m.shape[0]
    lane = lax.broadcasted_iota(jnp.int32, m.shape, 1)
    row = lax.broadcasted_iota(jnp.int32, m.shape, 0)
    turned = pltpu.roll(m, 1, axis=1)
    before = jnp.where(lane == 0, pltpu.roll(turned, 1, axis=0), turned)
    fresh = (m != before) | ((lane == 0) & (row == 0))
    fresh_b = as_bf16(fresh)
    upto = lax.broadcasted_iota(jnp.int32, (LANES, LANES), 0) <= lax.broadcasted_iota(
        jnp.int32, (LANES, LANES), 1
    )
    inside = dot(fresh_b, as_bf16(upto))
    totals = jnp.broadcast_to(inside[:, LANES - 1 :], inside.shape).astype(BF16)
    above = lax.broadcasted_iota(jnp.int32, (rows, rows), 1) < lax.broadcasted_iota(
        jnp.int32, (rows, rows), 0
    )
    rank = (inside + dot(as_bf16(above), totals)).astype(jnp.int32) - 1
    slot = rank
    local = m
    fresh_i = fresh.astype(jnp.int32)
    for o in range(1, owners):
        past = m >= o * mesh_dev
        start = jnp.sum(
            jnp.sum(jnp.where(past, 0, fresh_i), axis=0, keepdims=True), axis=1, keepdims=True
        )
        slot = jnp.where(past, rank + (o * CAP - start), slot)
        local = jnp.where(past, m - o * mesh_dev, local)
    slot_ref[...] = slot
    value = jnp.where(fresh, local + 1, 0)
    found = []
    for o in range(owners):
        places = o * CAP + lax.broadcasted_iota(jnp.int32, (CAP, LANES), 0)
        total = jnp.zeros((CAP, LANES), jnp.int32)
        for r in range(rows):
            total = total + jnp.where(slot[r : r + 1, :] == places, value[r : r + 1, :], 0)
        found.append(total)
    pad = jnp.zeros((LANES - CAP, LANES), jnp.int32)
    for o in range(owners):
        square = jnp.transpose(jnp.concatenate([found[o], pad], axis=0))
        ids_ref[o : o + 1, :] = jnp.sum(square, axis=0, keepdims=True) - 1


def node_pre_kernel(ml_ref, cot_ref, ws_ref, bn_ref, wno_ref, self_ref, cw_ref):
    self_ref[...] = dot(ml_ref[...], ws_ref[...]) + bn_ref[...]
    cw_ref[...] = dot_nt(cot_ref[...], wno_ref[...])


def hidden_kernel(gv_ref, win_ref, bin_ref, out_ref):
    v = dot(gv_ref[...], win_ref[...]) + bin_ref[...]
    out_ref[...] = (v * sigmoid(v)).astype(BF16)


def grid_kernel(ids_ref, hid_ref, wout_ref, gain_ref, ug_ref, lat_t_ref, out_ref, pg):
    @pl.when(pl.program_id(0) == 0)
    def _():
        out = dot(hid_ref[...], wout_ref[...])
        mean = jnp.mean(out, axis=-1, keepdims=True)
        centred = out - mean
        var = jnp.mean(centred * centred, axis=-1, keepdims=True)
        latent = centred * lax.rsqrt(var + 1e-05) * gain_ref[...]
        pg[...] = dot(latent.astype(BF16), ug_ref[...]).astype(BF16)
        lat_t_ref[...] = jnp.transpose(latent).astype(BF16)

    onehot = edges_by_ids(grid_block(ids_ref, pg.shape[0]), pg.shape[0])
    out_ref[...] = dot(onehot, pg[...]).astype(BF16)


def take_latent_kernel(ids_ref, lat_t_ref, out_ref):
    onehot = ids_by_edges(grid_block(ids_ref, lat_t_ref.shape[1]), lat_t_ref.shape[1])
    out_ref[...] = dot(lat_t_ref[...], onehot).astype(BF16)


def ask_kernel(ids_ref, ml_ref, asked_ref, onehot_ref):
    owners = ids_ref.shape[0]
    nodes = ml_ref.shape[0]
    columns = jnp.transpose(ids_ref[...])
    lanes = lax.broadcasted_iota(jnp.int32, (CAP, nodes), 1)
    onehot = jnp.concatenate(
        [as_bf16(columns[:CAP, o : o + 1] == lanes) for o in range(owners)], axis=0
    )
    onehot_ref[...] = onehot
    asked_ref[...] = dot(onehot, ml_ref[...]).astype(BF16)


def pre_of(slot, pm, pg, bias):
    return dot(edges_by_ids(slot, pm.shape[0]), pm) + pg.astype(F32) + bias


def edge_kernel(steps, slot_ref, pg_ref, ml_ref, um_ref, be_ref, we_ref, sums_ref, act_ref, pm_ref, total):
    step = pl.program_id(0)

    @pl.when(step == 0)
    def _():
        total[...] = jnp.zeros_like(total)
        pm_ref[...] = dot(ml_ref[...], um_ref[...]).astype(BF16)

    slot = slot_ref[...]
    pre = pre_of(slot, pm_ref[...], pg_ref[...], be_ref[...])
    act = (pre * sigmoid(pre)).astype(BF16)
    total[...] += dot(ids_by_edges(slot, total.shape[0]), act)

    @pl.when(step == steps - 1)
    def _():
        sums = total[...]
        high = sums.astype(BF16)
        low = (sums - high.astype(F32)).astype(BF16)
        act_ref[...] = high
        sums_ref[...] = (dot(high, we_ref[...]) + dot(low, we_ref[...])).astype(BF16)


def slope_kernel(slot_ref, pg_ref, pm_ref, be_ref, slope_ref, total_ref):
    @pl.when(pl.program_id(0) == 0)
    def _():
        total_ref[...] = jnp.zeros_like(total_ref)

    slot = slot_ref[...]
    pre = pre_of(slot, pm_ref[...], pg_ref[...], be_ref[...])
    s = sigmoid(pre)
    slope = (s * (1.0 + pre * (1.0 - s))).astype(BF16)
    slope_ref[...] = slope
    total_ref[...] += dot(ids_by_edges(slot, total_ref.shape[0]), slope)


def owned(row_ref, rec_ref, nodes):
    places = lax.broadcasted_iota(jnp.int32, (nodes, row_ref.shape[1]), 0)
    return dot(as_bf16(places == row_ref[...]), rec_ref[...]).astype(BF16)


def node_kernel(rec_ref, row_ref, oh_ref, self_ref, cw_ref, wa_ref, gask_ref, gnode_ref, nact_ref):
    agg = owned(row_ref, rec_ref, self_ref.shape[0])
    pre = self_ref[...] + dot(agg, wa_ref[...])
    s = sigmoid(pre)
    g_node = (cw_ref[...] * (s * (1.0 + pre * (1.0 - s)))).astype(BF16)
    g_agg = dot_nt(g_node, wa_ref[...]).astype(BF16)
    gask_ref[...] = dot(oh_ref[...], g_agg).astype(BF16)
    gnode_ref[...] = g_node
    nact_ref[...] = (pre * s).astype(BF16)


def slot_grad_kernel(gc_ref, we_ref, slope_ref, gsum_ref, h_ref):
    h = dot_nt(gc_ref[...], we_ref[...])
    h_ref[...] = h.astype(BF16)
    gsum_ref[...] = (h * slope_ref[...]).astype(BF16)


def node_post_kernel(
    rec_ref, row_ref, gnode_ref, nact_ref, ml_ref, cot_ref, wno_ref, ws_ref, um_ref, mo_ref, gm_ref
):
    g_pmesh = owned(row_ref, rec_ref, ml_ref.shape[0])
    mo_ref[...] = (ml_ref[...].astype(F32) + dot(nact_ref[...], wno_ref[...])).astype(BF16)
    gm_ref[...] = (
        cot_ref[...].astype(F32) + dot_nt(gnode_ref[...], ws_ref[...]) + dot_nt(g_pmesh, um_ref[...])
    ).astype(BF16)


def put_halves(place, value, keep_ref, give_ref):
    core = lax.axis_index("core")
    half = value.shape[0] // 2

    @pl.when(core == 0)
    def _():
        keep_ref[place] = value[:half]
        give_ref[place] = value[half:]

    @pl.when(core != 0)
    def _():
        keep_ref[place] = value[half:]
        give_ref[place] = value[:half]


def edge_back_kernel(
    steps, slot_ref, slope_ref, lat_t_ref, h_ref, gsum_ref, ml_ref, gc_ref, act_ref, keep_ref, give_ref, total
):
    step = pl.program_id(0)

    @pl.when(step == 0)
    def _():
        total[...] = jnp.zeros_like(total)

    onehot = edges_by_ids(slot_ref[...], h_ref.shape[0])
    g_edge = (dot(onehot, h_ref[...]) * slope_ref[...].astype(F32)).astype(BF16)
    total[...] += dot(lat_t_ref[...], g_edge)

    @pl.when(step == steps - 1)
    def _():
        put_halves(0, total[...].astype(BF16), keep_ref, give_ref)
        put_halves(1, dot_tn(act_ref[...], gc_ref[...]).astype(BF16), keep_ref, give_ref)
        put_halves(2, dot_tn(ml_ref[...], gsum_ref[...]).astype(BF16), keep_ref, give_ref)


def parts_kernel(keep_ref, got_ref, out_ref):
    count, _, width = out_ref.shape
    low = keep_ref.shape[1] // count
    for i in range(keep_ref.shape[0]):
        both = (keep_ref[i].astype(F32) + got_ref[i].astype(F32)).astype(BF16)
        out_ref[:, i * low : (i + 1) * low] = both.reshape(count, low, width)


def spread_kernel(scale, parts_ref, out_ref):
    total = (jnp.sum(parts_ref[...].astype(F32), axis=0) * scale).astype(BF16)
    out_ref[...] = jnp.broadcast_to(total[None], out_ref.shape)


def finish_kernel(mine_ref, other_ref, *out_refs):
    count, rows, width = mine_ref.shape
    low = rows // len(out_refs)
    half = count * low
    core = lax.axis_index("core")

    def put(upper_ref, lower_ref):
        for i, out_ref in enumerate(out_refs):
            piece = slice(i * low, (i + 1) * low)
            out_ref[:half] = upper_ref[:, piece].astype(F32).reshape(half, width)
            out_ref[half:] = lower_ref[:, piece].astype(F32).reshape(half, width)

    @pl.when(core == 0)
    def _():
        put(mine_ref, other_ref)

    @pl.when(core != 0)
    def _():
        put(other_ref, mine_ref)


def other_core(value):
    return lax.ppermute(value, "core", [(0, 1), (1, 0)])


def held(value, after):
    def body(*refs):
        pass

    anywhere = pl.BlockSpec(memory_space=pl.ANY)
    return pl.pallas_call(
        body,
        out_shape=jax.ShapeDtypeStruct(value.shape, value.dtype),
        in_specs=[anywhere] * (1 + len(after)),
        out_specs=anywhere,
        input_output_aliases={0: 0},
        name="held",
    )(value, *after)


def shards(
    grid_vars,
    mesh_latent,
    cotangent,
    edge_grid,
    edge_mesh,
    w_in,
    b_in,
    w_out,
    norm_gain,
    u_grid,
    u_mesh,
    b_edge,
    w_edge,
    w_self,
    w_agg,
    b_node,
    w_node_out,
):
    grid_dev, variables = grid_vars.shape
    mesh_dev, width = mesh_latent.shape
    edge_dev = edge_grid.shape[0]
    owners = lax.axis_size("mesh")
    slots = owners * CAP
    rows = edge_dev // LANES
    block = ROWS * LANES
    steps = edge_dev // block
    scale = (edge_dev * lax.axis_size("x") * lax.axis_size("core") * owners) ** (-0.5)
    sds = jax.ShapeDtypeStruct

    def exchange(value):
        return lax.all_to_all(value, "mesh", 0, 0, tiled=True)

    grid_ids = edge_grid.reshape(rows, LANES)
    slot, ids = call(
        functools.partial(prep_kernel, owners, mesh_dev),
        "prep",
        [sds((rows, LANES), jnp.int32), sds((owners, LANES), jnp.int32)],
        [edge_mesh.reshape(rows, LANES)],
        1e9,
    )
    incoming = exchange(ids)

    tile = min(256, grid_dev)
    grid_spec = pl.BlockSpec((tile, width), lambda i: (i, 0))
    (hidden,) = call(
        hidden_kernel,
        "hidden",
        [sds((grid_dev, width), BF16)],
        [grid_vars, w_in, b_in.reshape(1, width)],
        2 * grid_dev * width * variables,
        grid=(grid_dev // tile,),
        in_specs=[
            pl.BlockSpec((tile, variables), lambda i: (i, 0)),
            whole((variables, width)),
            whole((1, width)),
        ],
        out_specs=[grid_spec],
        after=[ids],
    )

    node_f, node_b = sds((mesh_dev, width), F32), sds((mesh_dev, width), BF16)
    self_part, cot_part = call(
        node_pre_kernel,
        "node_pre",
        [node_f, node_f],
        [mesh_latent, cotangent, w_self, b_node.reshape(1, width), w_node_out],
        4 * mesh_dev * width * width,
        vmem=52,
        after=[hidden],
    )
    asked, onehot_in = call(
        ask_kernel,
        "ask",
        [sds((slots, width), BF16), sds((slots, mesh_dev), BF16)],
        [incoming, mesh_latent],
        2 * slots * mesh_dev * width,
        after=[self_part],
    )
    incoming_row = incoming[:, :CAP].reshape(1, slots)
    slot_latent = exchange(asked)

    id_spec = pl.BlockSpec((ROWS, LANES), lambda i: (i, 0))
    edge_spec = pl.BlockSpec((block, width), lambda i: (i, 0))
    edge_t_spec = pl.BlockSpec((width, block), lambda i: (0, i))
    latent_t, edge_pgrid = call(
        grid_kernel,
        "grid",
        [sds((width, grid_dev), BF16), sds((edge_dev, width), BF16)],
        [grid_ids, hidden, w_out, norm_gain.reshape(1, width), u_grid],
        4 * grid_dev * width * width + 2 * edge_dev * grid_dev * width,
        grid=(steps,),
        in_specs=[
            id_spec, whole((grid_dev, width)), whole((width, width)), whole((1, width)),
            whole((width, width)),
        ],
        out_specs=[whole((width, grid_dev)), edge_spec],
        scratch=[pltpu.VMEM((grid_dev, width), BF16)],
        vmem=52,
        after=[asked],
    )

    slots_b, slots_f = sds((slots, width), BF16), sds((slots, width), F32)
    slots_spec = whole((slots, width))
    mesh_spec = whole((mesh_dev, width))
    weight_spec = whole((width, width))
    row_spec = whole((1, slots))
    bias = b_edge.reshape(1, width)
    sums, act_sums, slot_pmesh = call(
        functools.partial(edge_kernel, steps),
        "edge",
        [slots_b, slots_b, slots_b],
        [slot, edge_pgrid, slot_latent, u_mesh, bias, w_edge],
        4 * edge_dev * slots * width + 6 * slots * width * width,
        grid=(steps,),
        in_specs=[id_spec, edge_spec, slots_spec, weight_spec, whole((1, width)), weight_spec],
        out_specs=[slots_spec, slots_spec, slots_spec],
        scratch=[pltpu.VMEM((slots, width), F32)],
        vmem=52,
    )
    received = exchange(sums)

    slope, slope_sums = call(
        slope_kernel,
        "slope",
        [sds((edge_dev, width), BF16), slots_f],
        [slot, edge_pgrid, slot_pmesh, bias],
        4 * edge_dev * slots * width,
        grid=(steps,),
        in_specs=[id_spec, edge_spec, slots_spec, whole((1, width))],
        out_specs=[edge_spec, slots_spec],
        vmem=52,
        after=[sums],
    )
    g_asked, g_node, node_act = call(
        node_kernel,
        "node",
        [slots_b, node_b, node_b],
        [received, incoming_row, onehot_in, self_part, cot_part, w_agg],
        4 * mesh_dev * width * width + 4 * mesh_dev * slots * width,
        vmem=52,
        after=[slope_sums],
    )
    slot_g = exchange(g_asked)

    (edge_latent_t,) = call(
        take_latent_kernel,
        "take_latent",
        [sds((width, edge_dev), BF16)],
        [grid_ids, latent_t],
        2 * edge_dev * grid_dev * width,
        grid=(steps,),
        in_specs=[id_spec, whole((width, grid_dev))],
        out_specs=[edge_t_spec],
        vmem=52,
        after=[g_asked],
    )
    half = width // 2
    gsum, h = call(
        slot_grad_kernel,
        "slot_grad",
        [slots_b, slots_b],
        [slot_g, w_edge, slope_sums],
        2 * slots * width * width,
        vmem=52,
        after=[edge_latent_t],
    )
    gsum_received = exchange(gsum)

    three = sds((3, half, width), BF16)
    keep, give = call(
        functools.partial(edge_back_kernel, steps),
        "edge_back",
        [three, three],
        [slot, slope, edge_latent_t, h, gsum, slot_latent, slot_g, act_sums],
        2 * edge_dev * (slots + width) * width + 4 * slots * width * width,
        grid=(steps,),
        in_specs=[id_spec, edge_spec, edge_t_spec] + [slots_spec] * 5,
        out_specs=[whole(three.shape), whole(three.shape)],
        scratch=[pltpu.VMEM((width, width), F32)],
        vmem=52,
    )
    others = ("x", "mesh")
    count = lax.axis_size("x") * owners
    pieces = sds((count, 3 * half // count, width), BF16)
    (parts,) = call(
        parts_kernel,
        "parts",
        [pieces],
        [keep, other_core(held(give, [gsum_received]))],
        3 * half * width,
    )
    summed = lax.all_to_all(parts, others, 0, 0, tiled=True)

    mesh_out, grad_mesh = call(
        node_post_kernel,
        "node_post",
        [node_b, node_b],
        [
            gsum_received, incoming_row, g_node, node_act, mesh_latent, cotangent,
            w_node_out, w_self, u_mesh,
        ],
        6 * mesh_dev * width * width + 2 * mesh_dev * slots * width,
        vmem=52,
        after=[parts],
    )
    (copies,) = call(
        functools.partial(spread_kernel, scale),
        "spread",
        [pieces],
        [summed],
        3 * half * width,
        after=[mesh_out],
    )
    mine = lax.all_to_all(copies, others, 0, 0, tiled=True)
    weight = sds((width, width), F32)
    grad_ugrid, grad_edge, grad_umesh = call(
        finish_kernel, "finish", [weight] * 3, [mine, other_core(mine)], 3 * width * width
    )
    return mesh_out, grad_mesh, grad_edge, grad_ugrid, grad_umesh


def solution(mesh):
    bands, owners = mesh.shape["band"], mesh.shape["mesh"]
    cores = 2
    fine = Mesh(mesh.devices.reshape(bands // cores, cores, owners), ("x", "core", "mesh"))
    split = ("x", "core", "mesh")
    return jax.shard_map(
        shards,
        mesh=fine,
        in_specs=(P(split, None),) * 3 + (P(split),) * 2 + (P(),) * 12,
        out_specs=(P(split, None), P(split, None), P(), P(), P()),
        check_vma=False,
    )
```

```python
import functools
import math

import jax
import jax.numpy as jnp
from jax import lax
from jax.experimental import pallas as pl
from jax.experimental.pallas import tpu as pltpu
from jax.sharding import Mesh
from jax.sharding import PartitionSpec as P

CAP = 48
LANES = 128
ROWS = 8
BF16 = jnp.bfloat16
F32 = jnp.float32


def dot(a, b):
    return jnp.dot(a, b, preferred_element_type=F32)


def dot_nt(a, b):
    return lax.dot_general(a, b, (((1,), (1,)), ((), ())), preferred_element_type=F32)


def sigmoid(v):
    return 0.5 + 0.5 * jnp.tanh(0.5 * v)


def as_bf16(mask, one=1.0):
    return jnp.where(mask, one, 0.0).astype(BF16)


def edges_by_ids(ids, count, one=1.0):
    columns = jnp.transpose(ids)
    lanes = lax.broadcasted_iota(jnp.int32, (LANES, count), 1)
    return jnp.concatenate(
        [as_bf16(columns[:, j : j + 1] == lanes, one) for j in range(ids.shape[0])], axis=0
    )


def ids_by_edges(ids, count):
    places = lax.broadcasted_iota(jnp.int32, (count, LANES), 0)
    return jnp.concatenate(
        [as_bf16(ids[j : j + 1, :] == places) for j in range(ids.shape[0])], axis=1
    )


def call(kernel, name, out, args, flops, grid=None, in_specs=None, out_specs=None, scratch=(), vmem=16, after=(), token=False):
    moved = sum(math.prod(a.shape) * a.dtype.itemsize for a in [*args, *out])
    count, last = len(args), len(args) + len(after) + len(out)

    def body(*refs):
        kernel(*refs[:count], *refs[count + len(after) : last], *refs[last + token :])
        if token:
            refs[last][...] = jnp.zeros_like(refs[last])

    if out_specs is None:
        out_specs = [pl.BlockSpec(memory_space=pltpu.VMEM)] * len(out)
    if token:
        out = [*out, jax.ShapeDtypeStruct((8, LANES), jnp.int32)]
        out_specs = [*out_specs, pl.BlockSpec((8, LANES), lambda *_: (0, 0))]
    if in_specs is None:
        in_specs = [pl.BlockSpec(memory_space=pltpu.VMEM)] * count
    extra = {} if grid is None else dict(grid=grid)
    return pl.pallas_call(
        body,
        out_shape=out,
        in_specs=list(in_specs) + [pl.BlockSpec(memory_space=pl.ANY)] * len(after),
        out_specs=out_specs,
        scratch_shapes=scratch,
        name=name,
        cost_estimate=pl.CostEstimate(flops=int(flops), bytes_accessed=int(moved), transcendentals=0),
        compiler_params=pltpu.CompilerParams(vmem_limit_bytes=vmem << 20),
        **extra,
    )(*args, *after)


def whole(shape):
    return pl.BlockSpec(shape, lambda i: (0,) * len(shape))


def band_index():
    return lax.axis_index("x") * lax.axis_size("core") + lax.axis_index("core")


def grid_block(ids_ref, count):
    device = band_index() * lax.axis_size("mesh") + lax.axis_index("mesh")
    return ids_ref[...] - device * count


def prep_kernel(owners, mesh_dev, em_ref, slot_ref, ids_ref):
    m = em_ref[...] - band_index() * (owners * mesh_dev)
    rows = m.shape[0]
    lane = lax.broadcasted_iota(jnp.int32, m.shape, 1)
    row = lax.broadcasted_iota(jnp.int32, m.shape, 0)
    turned = pltpu.roll(m, 1, axis=1)
    before = jnp.where(lane == 0, pltpu.roll(turned, 1, axis=0), turned)
    fresh = (m != before) | ((lane == 0) & (row == 0))
    fresh_b = as_bf16(fresh)
    upto = lax.broadcasted_iota(jnp.int32, (LANES, LANES), 0) <= lax.broadcasted_iota(
        jnp.int32, (LANES, LANES), 1
    )
    inside = dot(fresh_b, as_bf16(upto))
    totals = jnp.broadcast_to(inside[:, LANES - 1 :], inside.shape).astype(BF16)
    above = lax.broadcasted_iota(jnp.int32, (rows, rows), 1) < lax.broadcasted_iota(
        jnp.int32, (rows, rows), 0
    )
    rank = (inside + dot(as_bf16(above), totals)).astype(jnp.int32) - 1
    slot = rank
    local = m
    fresh_i = fresh.astype(jnp.int32)
    for o in range(1, owners):
        past = m >= o * mesh_dev
        start = jnp.sum(
            jnp.sum(jnp.where(past, 0, fresh_i), axis=0, keepdims=True), axis=1, keepdims=True
        )
        slot = jnp.where(past, rank + (o * CAP - start), slot)
        local = jnp.where(past, m - o * mesh_dev, local)
    slot_ref[...] = slot
    value = jnp.where(fresh, local + 1, 0)
    found = []
    for o in range(owners):
        places = o * CAP + lax.broadcasted_iota(jnp.int32, (CAP, LANES), 0)
        total = jnp.zeros((CAP, LANES), jnp.int32)
        for r in range(rows):
            total = total + jnp.where(slot[r : r + 1, :] == places, value[r : r + 1, :], 0)
        found.append(total)
    pad = jnp.zeros((LANES - CAP, LANES), jnp.int32)
    for o in range(owners):
        square = jnp.transpose(jnp.concatenate([found[o], pad], axis=0))
        ids_ref[o : o + 1, :] = jnp.sum(square, axis=0, keepdims=True) - 1


def node_pre_kernel(ml_ref, cot_ref, ws_ref, bn_ref, wno_ref, self_ref, cw_ref):
    self_ref[...] = dot(ml_ref[...], ws_ref[...]) + bn_ref[...]
    cw_ref[...] = dot_nt(cot_ref[...], wno_ref[...])


def hidden_kernel(gv_ref, win_ref, bin_ref, out_ref):
    v = dot(gv_ref[...], win_ref[...]) + bin_ref[...]
    out_ref[...] = (v * sigmoid(v)).astype(BF16)


def grid_kernel(ids_ref, hid_ref, wout_ref, gain_ref, ug_ref, lat_t_ref, out_ref, pg):
    @pl.when(pl.program_id(0) == 0)
    def _():
        out = dot(hid_ref[...], wout_ref[...])
        mean = jnp.mean(out, axis=-1, keepdims=True)
        centred = out - mean
        var = jnp.mean(centred * centred, axis=-1, keepdims=True)
        latent = centred * lax.rsqrt(var + 1e-05) * gain_ref[...]
        pg[...] = dot(latent.astype(BF16), ug_ref[...]).astype(BF16)
        lat_t_ref[...] = jnp.transpose(latent).astype(BF16)

    onehot = edges_by_ids(grid_block(ids_ref, pg.shape[0]), pg.shape[0], 0.5)
    out_ref[...] = dot(onehot, pg[...]).astype(BF16)


def take_latent_kernel(ids_ref, lat_t_ref, act_ref, ml_ref, out_ref, act_t_ref, ml_t_ref):
    @pl.when(pl.program_id(0) == 0)
    def _():
        act_t_ref[...] = jnp.transpose(act_ref[...])
        ml_t_ref[...] = jnp.transpose(ml_ref[...])

    onehot = ids_by_edges(grid_block(ids_ref, lat_t_ref.shape[1]), lat_t_ref.shape[1])
    out_ref[...] = dot(lat_t_ref[...], onehot).astype(BF16)


def ask_kernel(ids_ref, ml_ref, asked_ref, onehot_ref):
    owners = ids_ref.shape[0]
    nodes = ml_ref.shape[0]
    columns = jnp.transpose(ids_ref[...])
    lanes = lax.broadcasted_iota(jnp.int32, (CAP, nodes), 1)
    onehot = jnp.concatenate(
        [as_bf16(columns[:CAP, o : o + 1] == lanes) for o in range(owners)], axis=0
    )
    onehot_ref[...] = onehot
    asked_ref[...] = dot(onehot, ml_ref[...]).astype(BF16)


def half_pre(slot, pm, half_pg, bias):
    return dot(edges_by_ids(slot, pm.shape[0], 0.5), pm) + half_pg.astype(F32) + 0.5 * bias


def edge_kernel(steps, slot_ref, pg_ref, ml_ref, um_ref, be_ref, we_ref, sums_ref, act_ref, pm_ref, total):
    step = pl.program_id(0)

    @pl.when(step == 0)
    def _():
        total[...] = jnp.zeros_like(total)
        pm_ref[...] = dot(ml_ref[...], um_ref[...]).astype(BF16)

    slot = slot_ref[...]
    v = half_pre(slot, pm_ref[...], pg_ref[...], be_ref[...])
    act = (v + v * jnp.tanh(v)).astype(BF16)
    total[...] += dot(ids_by_edges(slot, total.shape[0]), act)

    @pl.when(step == steps - 1)
    def _():
        sums = total[...]
        high = sums.astype(BF16)
        low = (sums - high.astype(F32)).astype(BF16)
        act_ref[...] = high
        sums_ref[...] = (dot(high, we_ref[...]) + dot(low, we_ref[...])).astype(BF16)


def slope_kernel(slot_ref, pg_ref, pm_ref, be_ref, slope_ref, total_ref):
    @pl.when(pl.program_id(0) == 0)
    def _():
        total_ref[...] = jnp.zeros_like(total_ref)

    slot = slot_ref[...]
    v = half_pre(slot, pm_ref[...], pg_ref[...], be_ref[...])
    t = jnp.tanh(v)
    slope = ((1.0 + t) * (1.0 + v * (1.0 - t))).astype(BF16)
    slope_ref[...] = slope
    total_ref[...] += dot(ids_by_edges(slot, total_ref.shape[0]), slope)


def owned(row_ref, rec_ref, nodes):
    places = lax.broadcasted_iota(jnp.int32, (nodes, row_ref.shape[1]), 0)
    return dot(as_bf16(places == row_ref[...]), rec_ref[...]).astype(BF16)


def load(pairs, sems):
    copies = [pltpu.make_async_copy(a, b, sems.at[i]) for i, (a, b) in enumerate(pairs)]
    for copy in copies:
        copy.start()
    return copies


def node_kernel(
    rec_ref, row_ref, oh_hbm, self_hbm, cw_hbm, wa_hbm, gask_ref, gnode_ref, nact_ref,
    oh_ref, self_ref, cw_ref, wa_ref, sems,
):
    pairs = [(wa_hbm, wa_ref), (self_hbm, self_ref), (cw_hbm, cw_ref), (oh_hbm, oh_ref)]
    wa, own, cw, oh = load(pairs, sems)
    agg = owned(row_ref, rec_ref, self_ref.shape[0])
    wa.wait()
    pre = dot(agg, wa_ref[...])
    own.wait()
    pre = self_ref[...] + pre
    s = sigmoid(pre)
    cw.wait()
    g_node = (cw_ref[...] * (s * (1.0 + pre * (1.0 - s)))).astype(BF16)
    g_agg = dot_nt(g_node, wa_ref[...]).astype(BF16)
    oh.wait()
    gask_ref[...] = dot(oh_ref[...], g_agg).astype(BF16)
    gnode_ref[...] = g_node
    nact_ref[...] = (pre * s).astype(BF16)


def slot_grad_kernel(gc_ref, we_ref, slope_ref, gsum_ref, h_ref):
    h = 0.5 * dot_nt(gc_ref[...], we_ref[...])
    h_ref[...] = h.astype(BF16)
    gsum_ref[...] = (h * slope_ref[...]).astype(BF16)


def node_post_kernel(
    rec_ref, row_ref, gnode_ref, nact_ref, ml_ref, cot_ref, wno_ref, ws_ref, um_ref, mo_ref, gm_ref
):
    g_pmesh = owned(row_ref, rec_ref, ml_ref.shape[0])
    mo_ref[...] = (ml_ref[...].astype(F32) + dot(nact_ref[...], wno_ref[...])).astype(BF16)
    gm_ref[...] = (
        cot_ref[...].astype(F32) + dot_nt(gnode_ref[...], ws_ref[...]) + dot_nt(g_pmesh, um_ref[...])
    ).astype(BF16)


def put_halves(place, value, keep_ref, give_ref):
    core = lax.axis_index("core")
    half = value.shape[0] // 2

    @pl.when(core == 0)
    def _():
        keep_ref[place] = value[:half]
        give_ref[place] = value[half:]

    @pl.when(core != 0)
    def _():
        keep_ref[place] = value[half:]
        give_ref[place] = value[:half]


def edge_back_kernel(
    steps, slot_ref, slope_ref, lat_t_ref, h_ref, gsum_hbm, ml_hbm, gc_hbm, act_hbm, keep_ref, give_ref,
    total, gsum_ref, ml_ref, gc_ref, act_ref, sems,
):
    step = pl.program_id(0)
    late = [(act_hbm, act_ref), (gc_hbm, gc_ref), (ml_hbm, ml_ref), (gsum_hbm, gsum_ref)]

    @pl.when(step == 0)
    def _():
        total[...] = jnp.zeros_like(total)
        load(late, sems)

    onehot = edges_by_ids(slot_ref[...], h_ref.shape[0])
    g_edge = (dot(onehot, h_ref[...]) * slope_ref[...].astype(F32)).astype(BF16)
    total[...] += dot(lat_t_ref[...], g_edge)

    @pl.when(step == steps - 1)
    def _():
        for i, (a, b) in enumerate(late):
            pltpu.make_async_copy(a, b, sems.at[i]).wait()
        put_halves(0, total[...].astype(BF16), keep_ref, give_ref)
        put_halves(1, dot(act_ref[...], gc_ref[...]).astype(BF16), keep_ref, give_ref)
        put_halves(2, dot(ml_ref[...], gsum_ref[...]).astype(BF16), keep_ref, give_ref)


def parts_kernel(keep_ref, got_ref, out_ref):
    count, _, width = out_ref.shape
    low = keep_ref.shape[1] // count
    for i in range(keep_ref.shape[0]):
        both = (keep_ref[i].astype(F32) + got_ref[i].astype(F32)).astype(BF16)
        out_ref[:, i * low : (i + 1) * low] = both.reshape(count, low, width)


def spread_kernel(scale, parts_ref, out_ref):
    total = (jnp.sum(parts_ref[...].astype(F32), axis=0) * scale).astype(BF16)
    out_ref[...] = jnp.broadcast_to(total[None], out_ref.shape)


def finish_kernel(mine_ref, other_ref, *out_refs):
    count, rows, width = mine_ref.shape
    low = rows // len(out_refs)
    half = count * low
    core = lax.axis_index("core")

    def put(upper_ref, lower_ref):
        for i, out_ref in enumerate(out_refs):
            piece = slice(i * low, (i + 1) * low)
            out_ref[:half] = upper_ref[:, piece].astype(F32).reshape(half, width)
            out_ref[half:] = lower_ref[:, piece].astype(F32).reshape(half, width)

    @pl.when(core == 0)
    def _():
        put(mine_ref, other_ref)

    @pl.when(core != 0)
    def _():
        put(other_ref, mine_ref)


def other_core(value):
    return lax.ppermute(value, "core", [(0, 1), (1, 0)])


def held(value, after):
    def body(*refs):
        pass

    anywhere = pl.BlockSpec(memory_space=pl.ANY)
    return pl.pallas_call(
        body,
        out_shape=jax.ShapeDtypeStruct(value.shape, value.dtype),
        in_specs=[anywhere] * (1 + len(after)),
        out_specs=anywhere,
        input_output_aliases={0: 0},
        name="held",
        compiler_params=pltpu.CompilerParams(vmem_limit_bytes=60 << 20),
    )(value, *after)


def shards(
    grid_vars,
    mesh_latent,
    cotangent,
    edge_grid,
    edge_mesh,
    w_in,
    b_in,
    w_out,
    norm_gain,
    u_grid,
    u_mesh,
    b_edge,
    w_edge,
    w_self,
    w_agg,
    b_node,
    w_node_out,
):
    grid_dev, variables = grid_vars.shape
    mesh_dev, width = mesh_latent.shape
    edge_dev = edge_grid.shape[0]
    owners = lax.axis_size("mesh")
    slots = owners * CAP
    rows = edge_dev // LANES
    block = ROWS * LANES
    steps = edge_dev // block
    scale = (edge_dev * lax.axis_size("x") * lax.axis_size("core") * owners) ** (-0.5)
    sds, hbm = jax.ShapeDtypeStruct, pltpu.HBM

    def exchange(value):
        return lax.all_to_all(value, "mesh", 0, 0, tiled=True)

    grid_ids = edge_grid.reshape(rows, LANES)
    slot, ids = call(
        functools.partial(prep_kernel, owners, mesh_dev),
        "prep",
        [sds((rows, LANES), jnp.int32), sds((owners, LANES), jnp.int32)],
        [edge_mesh.reshape(rows, LANES)],
        1e9,
    )
    incoming = exchange(ids)

    tile = min(256, grid_dev)
    grid_spec = pl.BlockSpec((tile, width), lambda i: (i, 0))
    hidden, hidden_done = call(
        hidden_kernel,
        "hidden",
        [hbm((grid_dev, width), BF16)],
        [grid_vars, w_in, b_in.reshape(1, width)],
        2 * grid_dev * width * variables,
        grid=(grid_dev // tile,),
        in_specs=[
            pl.BlockSpec((tile, variables), lambda i: (i, 0)),
            whole((variables, width)),
            whole((1, width)),
        ],
        out_specs=[grid_spec],
        after=[ids],
        token=True,
    )

    node_f, node_b = hbm((mesh_dev, width), F32), hbm((mesh_dev, width), BF16)
    self_part, cot_part, node_pre_done = call(
        node_pre_kernel,
        "node_pre",
        [node_f, node_f],
        [mesh_latent, cotangent, w_self, b_node.reshape(1, width), w_node_out],
        4 * mesh_dev * width * width,
        vmem=52,
        after=[hidden_done],
        token=True,
    )
    asked, onehot_in = call(
        ask_kernel,
        "ask",
        [sds((slots, width), BF16), sds((slots, mesh_dev), BF16)],
        [incoming, mesh_latent],
        2 * slots * mesh_dev * width,
        after=[node_pre_done],
    )
    incoming_row = incoming[:, :CAP].reshape(1, slots)
    slot_latent = exchange(asked)

    id_spec = pl.BlockSpec((ROWS, LANES), lambda i: (i, 0))
    edge_spec = pl.BlockSpec((block, width), lambda i: (i, 0))
    edge_t_spec = pl.BlockSpec((width, block), lambda i: (0, i))
    latent_t, edge_pgrid = call(
        grid_kernel,
        "grid",
        [sds((width, grid_dev), BF16), sds((edge_dev, width), BF16)],
        [grid_ids, hidden, w_out, norm_gain.reshape(1, width), u_grid],
        4 * grid_dev * width * width + 2 * edge_dev * grid_dev * width,
        grid=(steps,),
        in_specs=[
            id_spec, whole((grid_dev, width)), whole((width, width)), whole((1, width)),
            whole((width, width)),
        ],
        out_specs=[whole((width, grid_dev)), edge_spec],
        scratch=[pltpu.VMEM((grid_dev, width), BF16)],
        vmem=60,
        after=[asked],
    )

    slots_b, slots_h = sds((slots, width), BF16), hbm((slots, width), BF16)
    slots_spec = whole((slots, width))
    mesh_spec = whole((mesh_dev, width))
    weight_spec = whole((width, width))
    row_spec = whole((1, slots))
    bias = b_edge.reshape(1, width)
    sums, act_sums, slot_pmesh = call(
        functools.partial(edge_kernel, steps),
        "edge",
        [slots_b, slots_h, slots_h],
        [slot, edge_pgrid, slot_latent, u_mesh, bias, w_edge],
        4 * edge_dev * slots * width + 6 * slots * width * width,
        grid=(steps,),
        in_specs=[id_spec, edge_spec, slots_spec, weight_spec, whole((1, width)), weight_spec],
        out_specs=[slots_spec, slots_spec, slots_spec],
        scratch=[pltpu.VMEM((slots, width), F32)],
        vmem=52,
    )
    received = exchange(sums)

    slope, slope_sums, slope_done = call(
        slope_kernel,
        "slope",
        [hbm((edge_dev, width), BF16), hbm((slots, width), F32)],
        [slot, edge_pgrid, slot_pmesh, bias],
        4 * edge_dev * slots * width,
        grid=(steps,),
        in_specs=[id_spec, edge_spec, slots_spec, whole((1, width))],
        out_specs=[edge_spec, slots_spec],
        vmem=60,
        after=[sums],
        token=True,
    )
    g_asked, g_node, node_act = call(
        node_kernel,
        "node",
        [slots_b, node_b, node_b],
        [received, incoming_row, onehot_in, self_part, cot_part, w_agg],
        4 * mesh_dev * width * width + 4 * mesh_dev * slots * width,
        in_specs=[pl.BlockSpec(memory_space=pltpu.VMEM)] * 2 + [pl.BlockSpec(memory_space=pl.ANY)] * 4,
        scratch=[
            pltpu.VMEM((slots, mesh_dev), BF16),
            pltpu.VMEM((mesh_dev, width), F32),
            pltpu.VMEM((mesh_dev, width), F32),
            pltpu.VMEM((width, width), BF16),
            pltpu.SemaphoreType.DMA((4,)),
        ],
        vmem=60,
        after=[slope_done],
    )
    slot_g = exchange(g_asked)

    slots_t_spec = whole((width, slots))
    edge_latent_t, act_sums_t, slot_latent_t, take_done = call(
        take_latent_kernel,
        "take_latent",
        [hbm((width, edge_dev), BF16), hbm((width, slots), BF16), hbm((width, slots), BF16)],
        [grid_ids, latent_t, act_sums, slot_latent],
        2 * edge_dev * grid_dev * width,
        grid=(steps,),
        in_specs=[id_spec, whole((width, grid_dev)), slots_spec, slots_spec],
        out_specs=[edge_t_spec, slots_t_spec, slots_t_spec],
        vmem=52,
        after=[g_asked],
        token=True,
    )
    half = width // 2
    gsum, h = call(
        slot_grad_kernel,
        "slot_grad",
        [slots_h, slots_h],
        [slot_g, w_edge, slope_sums],
        2 * slots * width * width,
        vmem=52,
        after=[take_done],
    )
    gsum_received = exchange(gsum)

    three = hbm((3, half, width), BF16)
    keep, give = call(
        functools.partial(edge_back_kernel, steps),
        "edge_back",
        [three, three],
        [slot, slope, edge_latent_t, h, gsum, slot_latent_t, slot_g, act_sums_t],
        2 * edge_dev * (slots + width) * width + 4 * slots * width * width,
        grid=(steps,),
        in_specs=[id_spec, edge_spec, edge_t_spec, slots_spec] + [pl.BlockSpec(memory_space=pl.ANY)] * 4,
        out_specs=[whole(three.shape), whole(three.shape)],
        scratch=[pltpu.VMEM((width, width), F32)]
        + [pltpu.VMEM(a, BF16) for a in ((slots, width), (width, slots)) * 2]
        + [pltpu.SemaphoreType.DMA((4,))],
        vmem=60,
    )
    others = ("x", "mesh")
    count = lax.axis_size("x") * owners
    pieces = sds((count, 3 * half // count, width), BF16)
    (parts,) = call(
        parts_kernel,
        "parts",
        [pieces],
        [keep, other_core(held(give, [gsum_received]))],
        3 * half * width,
    )
    summed = lax.all_to_all(parts, others, 0, 0, tiled=True)

    mesh_out, grad_mesh, node_post_done = call(
        node_post_kernel,
        "node_post",
        [node_b, node_b],
        [
            gsum_received, incoming_row, g_node, node_act, mesh_latent, cotangent,
            w_node_out, w_self, u_mesh,
        ],
        6 * mesh_dev * width * width + 2 * mesh_dev * slots * width,
        vmem=52,
        after=[parts],
        token=True,
    )
    (copies,) = call(
        functools.partial(spread_kernel, scale),
        "spread",
        [pieces],
        [summed],
        3 * half * width,
        after=[node_post_done],
    )
    mine = lax.all_to_all(copies, others, 0, 0, tiled=True)
    weight = sds((width, width), F32)
    grad_ugrid, grad_edge, grad_umesh = call(
        finish_kernel, "finish", [weight] * 3, [mine, other_core(mine)], 3 * width * width
    )
    return mesh_out, grad_mesh, grad_edge, grad_ugrid, grad_umesh


def solution(mesh):
    bands, owners = mesh.shape["band"], mesh.shape["mesh"]
    cores = 2
    fine = Mesh(mesh.devices.reshape(bands // cores, cores, owners), ("x", "core", "mesh"))
    split = ("x", "core", "mesh")
    return jax.shard_map(
        shards,
        mesh=fine,
        in_specs=(P(split, None),) * 3 + (P(split),) * 2 + (P(),) * 12,
        out_specs=(P(split, None), P(split, None), P(), P(), P()),
        check_vma=False,
    )
```

```python
import functools
import math

import jax
import jax.numpy as jnp
from jax import lax
from jax.experimental import pallas as pl
from jax.experimental.pallas import tpu as pltpu
from jax.sharding import Mesh
from jax.sharding import PartitionSpec as P

CAP = 48
LANES = 128
ROWS = 8
BF16 = jnp.bfloat16
F32 = jnp.float32


def dot(a, b):
    return jnp.dot(a, b, preferred_element_type=F32)


def dot_nt(a, b):
    return lax.dot_general(a, b, (((1,), (1,)), ((), ())), preferred_element_type=F32)


def sigmoid(v):
    return 0.5 + 0.5 * jnp.tanh(0.5 * v)


def as_bf16(mask, one=1.0):
    return jnp.where(mask, one, 0.0).astype(BF16)


def edges_by_ids(ids, count, one=1.0):
    columns = jnp.transpose(ids)
    lanes = lax.broadcasted_iota(jnp.int32, (LANES, count), 1)
    return jnp.concatenate(
        [as_bf16(columns[:, j : j + 1] == lanes, one) for j in range(ids.shape[0])], axis=0
    )


def ids_by_edges(ids, count):
    places = lax.broadcasted_iota(jnp.int32, (count, LANES), 0)
    return jnp.concatenate(
        [as_bf16(ids[j : j + 1, :] == places) for j in range(ids.shape[0])], axis=1
    )


def call(kernel, name, out, args, flops, grid=None, in_specs=None, out_specs=None, scratch=(), vmem=16, after=(), token=False):
    moved = sum(math.prod(a.shape) * a.dtype.itemsize for a in [*args, *out])
    count, last = len(args), len(args) + len(after) + len(out)

    def body(*refs):
        kernel(*refs[:count], *refs[count + len(after) : last], *refs[last + token :])
        if token:
            refs[last][...] = jnp.zeros_like(refs[last])

    if out_specs is None:
        out_specs = [pl.BlockSpec(memory_space=pltpu.VMEM)] * len(out)
    if token:
        out = [*out, jax.ShapeDtypeStruct((8, LANES), jnp.int32)]
        out_specs = [*out_specs, pl.BlockSpec((8, LANES), lambda *_: (0, 0))]
    if in_specs is None:
        in_specs = [pl.BlockSpec(memory_space=pltpu.VMEM)] * count
    extra = {} if grid is None else dict(grid=grid)
    return pl.pallas_call(
        body,
        out_shape=out,
        in_specs=list(in_specs) + [pl.BlockSpec(memory_space=pl.ANY)] * len(after),
        out_specs=out_specs,
        scratch_shapes=scratch,
        name=name,
        cost_estimate=pl.CostEstimate(flops=int(flops), bytes_accessed=int(moved), transcendentals=0),
        compiler_params=pltpu.CompilerParams(vmem_limit_bytes=vmem << 20),
        **extra,
    )(*args, *after)


def whole(shape):
    return pl.BlockSpec(shape, lambda i: (0,) * len(shape))


def band_index():
    return lax.axis_index("x") * lax.axis_size("core") + lax.axis_index("core")


def grid_block(ids_ref, count):
    device = band_index() * lax.axis_size("mesh") + lax.axis_index("mesh")
    return ids_ref[...] - device * count


def prep_kernel(owners, mesh_dev, em_ref, slot_ref, ids_ref):
    m = em_ref[...] - band_index() * (owners * mesh_dev)
    rows = m.shape[0]
    lane = lax.broadcasted_iota(jnp.int32, m.shape, 1)
    row = lax.broadcasted_iota(jnp.int32, m.shape, 0)
    turned = pltpu.roll(m, 1, axis=1)
    before = jnp.where(lane == 0, pltpu.roll(turned, 1, axis=0), turned)
    fresh = (m != before) | ((lane == 0) & (row == 0))
    fresh_b = as_bf16(fresh)
    upto = lax.broadcasted_iota(jnp.int32, (LANES, LANES), 0) <= lax.broadcasted_iota(
        jnp.int32, (LANES, LANES), 1
    )
    inside = dot(fresh_b, as_bf16(upto))
    totals = jnp.broadcast_to(inside[:, LANES - 1 :], inside.shape).astype(BF16)
    above = lax.broadcasted_iota(jnp.int32, (rows, rows), 1) < lax.broadcasted_iota(
        jnp.int32, (rows, rows), 0
    )
    rank = (inside + dot(as_bf16(above), totals)).astype(jnp.int32) - 1
    slot = rank
    local = m
    fresh_i = fresh.astype(jnp.int32)
    for o in range(1, owners):
        past = m >= o * mesh_dev
        start = jnp.sum(
            jnp.sum(jnp.where(past, 0, fresh_i), axis=0, keepdims=True), axis=1, keepdims=True
        )
        slot = jnp.where(past, rank + (o * CAP - start), slot)
        local = jnp.where(past, m - o * mesh_dev, local)
    slot_ref[...] = slot
    value = jnp.where(fresh, local + 1, 0)
    found = []
    for o in range(owners):
        places = o * CAP + lax.broadcasted_iota(jnp.int32, (CAP, LANES), 0)
        total = jnp.zeros((CAP, LANES), jnp.int32)
        for r in range(rows):
            total = total + jnp.where(slot[r : r + 1, :] == places, value[r : r + 1, :], 0)
        found.append(total)
    pad = jnp.zeros((LANES - CAP, LANES), jnp.int32)
    for o in range(owners):
        square = jnp.transpose(jnp.concatenate([found[o], pad], axis=0))
        ids_ref[o : o + 1, :] = jnp.sum(square, axis=0, keepdims=True) - 1


def node_pre_kernel(ml_ref, cot_ref, ws_ref, bn_ref, wno_ref, self_ref, cw_ref):
    self_ref[...] = dot(ml_ref[...], ws_ref[...]) + bn_ref[...]
    cw_ref[...] = dot_nt(cot_ref[...], wno_ref[...])


def hidden_kernel(gv_ref, win_ref, bin_ref, out_ref):
    v = dot(gv_ref[...], win_ref[...]) + bin_ref[...]
    out_ref[...] = (v * sigmoid(v)).astype(BF16)


def grid_kernel(ids_ref, hid_ref, wout_ref, gain_ref, ug_ref, lat_t_ref, out_ref, pg):
    @pl.when(pl.program_id(0) == 0)
    def _():
        out = dot(hid_ref[...], wout_ref[...])
        mean = jnp.mean(out, axis=-1, keepdims=True)
        centred = out - mean
        var = jnp.mean(centred * centred, axis=-1, keepdims=True)
        latent = centred * lax.rsqrt(var + 1e-05) * gain_ref[...]
        pg[...] = dot(latent.astype(BF16), ug_ref[...]).astype(BF16)
        lat_t_ref[...] = jnp.transpose(latent).astype(BF16)

    onehot = edges_by_ids(grid_block(ids_ref, pg.shape[0]), pg.shape[0], 0.5)
    out_ref[...] = dot(onehot, pg[...]).astype(BF16)


def take_latent_kernel(ids_ref, lat_t_ref, act_ref, ml_ref, out_ref, act_t_ref, ml_t_ref):
    @pl.when(pl.program_id(0) == 0)
    def _():
        act_t_ref[...] = jnp.transpose(act_ref[...])
        ml_t_ref[...] = jnp.transpose(ml_ref[...])

    onehot = ids_by_edges(grid_block(ids_ref, lat_t_ref.shape[1]), lat_t_ref.shape[1])
    out_ref[...] = dot(lat_t_ref[...], onehot).astype(BF16)


def ask_kernel(ids_ref, ml_ref, asked_ref, onehot_ref):
    owners = ids_ref.shape[0]
    nodes = ml_ref.shape[0]
    columns = jnp.transpose(ids_ref[...])
    lanes = lax.broadcasted_iota(jnp.int32, (CAP, nodes), 1)
    onehot = jnp.concatenate(
        [as_bf16(columns[:CAP, o : o + 1] == lanes) for o in range(owners)], axis=0
    )
    onehot_ref[...] = onehot
    asked_ref[...] = dot(onehot, ml_ref[...]).astype(BF16)


def half_pre(slot, pm, half_pg, bias):
    return dot(edges_by_ids(slot, pm.shape[0], 0.5), pm) + half_pg.astype(F32) + 0.5 * bias


def edge_kernel(steps, slot_ref, pg_ref, ml_ref, um_ref, be_ref, we_ref, sums_ref, act_ref, pm_ref, total):
    step = pl.program_id(0)

    @pl.when(step == 0)
    def _():
        total[...] = jnp.zeros_like(total)
        pm_ref[...] = dot(ml_ref[...], um_ref[...]).astype(BF16)

    slot = slot_ref[...]
    v = half_pre(slot, pm_ref[...], pg_ref[...], be_ref[...])
    act = (v + v * jnp.tanh(v)).astype(BF16)
    total[...] += dot(ids_by_edges(slot, total.shape[0]), act)

    @pl.when(step == steps - 1)
    def _():
        sums = total[...]
        high = sums.astype(BF16)
        low = (sums - high.astype(F32)).astype(BF16)
        act_ref[...] = high
        sums_ref[...] = (dot(high, we_ref[...]) + dot(low, we_ref[...])).astype(BF16)


def slope_kernel(slot_ref, pg_ref, pm_ref, be_ref, slope_ref, total_ref):
    @pl.when(pl.program_id(0) == 0)
    def _():
        total_ref[...] = jnp.zeros_like(total_ref)

    slot = slot_ref[...]
    v = half_pre(slot, pm_ref[...], pg_ref[...], be_ref[...])
    t = jnp.tanh(v)
    slope = ((1.0 + t) * (1.0 + v * (1.0 - t))).astype(BF16)
    slope_ref[...] = slope
    total_ref[...] += dot(ids_by_edges(slot, total_ref.shape[0]), slope)


def owned(row_ref, rec_ref, nodes):
    places = lax.broadcasted_iota(jnp.int32, (nodes, row_ref.shape[1]), 0)
    return dot(as_bf16(places == row_ref[...]), rec_ref[...]).astype(BF16)


def load(pairs, sems):
    copies = [pltpu.make_async_copy(a, b, sems.at[i]) for i, (a, b) in enumerate(pairs)]
    for copy in copies:
        copy.start()
    return copies


def node_kernel(
    rec_ref, row_ref, oh_hbm, self_hbm, cw_hbm, wa_hbm, gask_ref, gnode_ref, nact_ref,
    oh_ref, self_ref, cw_ref, wa_ref, sems,
):
    pairs = [(wa_hbm, wa_ref), (self_hbm, self_ref), (cw_hbm, cw_ref), (oh_hbm, oh_ref)]
    wa, own, cw, oh = load(pairs, sems)
    agg = owned(row_ref, rec_ref, self_ref.shape[0])
    wa.wait()
    pre = dot(agg, wa_ref[...])
    own.wait()
    pre = self_ref[...] + pre
    s = sigmoid(pre)
    cw.wait()
    g_node = (cw_ref[...] * (s * (1.0 + pre * (1.0 - s)))).astype(BF16)
    g_agg = dot_nt(g_node, wa_ref[...]).astype(BF16)
    oh.wait()
    gask_ref[...] = dot(oh_ref[...], g_agg).astype(BF16)
    gnode_ref[...] = g_node
    nact_ref[...] = (pre * s).astype(BF16)


def slot_grad_kernel(gc_ref, we_ref, slope_ref, gsum_ref, h_ref):
    h = 0.5 * dot_nt(gc_ref[...], we_ref[...])
    h_ref[...] = h.astype(BF16)
    gsum_ref[...] = (h * slope_ref[...]).astype(BF16)


def node_post_kernel(
    rec_ref, row_ref, gnode_ref, nact_ref, ml_ref, cot_ref, wno_ref, ws_ref, um_ref, mo_ref, gm_ref
):
    g_pmesh = owned(row_ref, rec_ref, ml_ref.shape[0])
    mo_ref[...] = (ml_ref[...].astype(F32) + dot(nact_ref[...], wno_ref[...])).astype(BF16)
    gm_ref[...] = (
        cot_ref[...].astype(F32) + dot_nt(gnode_ref[...], ws_ref[...]) + dot_nt(g_pmesh, um_ref[...])
    ).astype(BF16)


def put_halves(place, value, keep_ref, give_ref):
    core = lax.axis_index("core")
    half = value.shape[0] // 2

    @pl.when(core == 0)
    def _():
        keep_ref[place] = value[:half]
        give_ref[place] = value[half:]

    @pl.when(core != 0)
    def _():
        keep_ref[place] = value[half:]
        give_ref[place] = value[:half]


def edge_back_kernel(
    steps, slot_ref, slope_ref, lat_t_ref, h_ref, gsum_hbm, ml_hbm, gc_hbm, act_hbm, keep_ref, give_ref,
    total, gsum_ref, ml_ref, gc_ref, act_ref, sems,
):
    step = pl.program_id(0)
    late = [(act_hbm, act_ref), (gc_hbm, gc_ref), (ml_hbm, ml_ref), (gsum_hbm, gsum_ref)]

    @pl.when(step == 0)
    def _():
        total[...] = jnp.zeros_like(total)
        load(late, sems)

    onehot = edges_by_ids(slot_ref[...], h_ref.shape[0])
    g_edge = (dot(onehot, h_ref[...]) * slope_ref[...].astype(F32)).astype(BF16)
    total[...] += dot(lat_t_ref[...], g_edge)

    @pl.when(step == steps - 1)
    def _():
        for i, (a, b) in enumerate(late):
            pltpu.make_async_copy(a, b, sems.at[i]).wait()
        put_halves(0, total[...].astype(BF16), keep_ref, give_ref)
        put_halves(1, dot(act_ref[...], gc_ref[...]).astype(BF16), keep_ref, give_ref)
        put_halves(2, dot(ml_ref[...], gsum_ref[...]).astype(BF16), keep_ref, give_ref)


def parts_kernel(keep_ref, got_ref, out_ref):
    count, _, width = out_ref.shape
    low = keep_ref.shape[1] // count
    for i in range(keep_ref.shape[0]):
        both = (keep_ref[i].astype(F32) + got_ref[i].astype(F32)).astype(BF16)
        out_ref[:, i * low : (i + 1) * low] = both.reshape(count, low, width)


def spread_kernel(scale, parts_ref, out_ref):
    total = (jnp.sum(parts_ref[...].astype(F32), axis=0) * scale).astype(BF16)
    out_ref[...] = jnp.broadcast_to(total[None], out_ref.shape)


def finish_kernel(ours, part_ref, *refs):
    *out_refs, rows_ref, sems = refs[-5:]
    count, rows, width = part_ref.shape
    low = rows // len(out_refs)
    half = count * low
    core = lax.axis_index("core")
    start = pl.multiple_of((core if ours else 1 - core) * half, half)
    copies = []
    for i, out_ref in enumerate(out_refs):
        piece = part_ref[:, i * low : (i + 1) * low]
        rows_ref[i] = piece.astype(F32).reshape(half, width)
        copies.append(pltpu.make_async_copy(rows_ref.at[i], out_ref.at[pl.ds(start, half)], sems.at[i]))
        copies[i].start()
    for copy in copies:
        copy.wait()


def finish(ours, part, width, before=()):
    anywhere = pl.BlockSpec(memory_space=pl.ANY)
    half = width // 2
    return pl.pallas_call(
        functools.partial(finish_kernel, ours),
        out_shape=[jax.ShapeDtypeStruct((width, width), F32)] * 3,
        in_specs=[pl.BlockSpec(memory_space=pltpu.VMEM)] + [anywhere] * len(before),
        out_specs=[anywhere] * 3,
        scratch_shapes=[pltpu.VMEM((3, half, width), F32), pltpu.SemaphoreType.DMA((3,))],
        input_output_aliases={i + 1: i for i in range(len(before))},
        name="finish_ours" if ours else "finish_other",
        cost_estimate=pl.CostEstimate(flops=3 * half * width, bytes_accessed=18 * half * width, transcendentals=0),
        compiler_params=pltpu.CompilerParams(vmem_limit_bytes=16 << 20),
    )(part, *before)


def other_core(value):
    return lax.ppermute(value, "core", [(0, 1), (1, 0)])


def held(value, after):
    def body(*refs):
        pass

    anywhere = pl.BlockSpec(memory_space=pl.ANY)
    return pl.pallas_call(
        body,
        out_shape=jax.ShapeDtypeStruct(value.shape, value.dtype),
        in_specs=[anywhere] * (1 + len(after)),
        out_specs=anywhere,
        input_output_aliases={0: 0},
        name="held",
        compiler_params=pltpu.CompilerParams(vmem_limit_bytes=60 << 20),
    )(value, *after)


def shards(
    grid_vars,
    mesh_latent,
    cotangent,
    edge_grid,
    edge_mesh,
    w_in,
    b_in,
    w_out,
    norm_gain,
    u_grid,
    u_mesh,
    b_edge,
    w_edge,
    w_self,
    w_agg,
    b_node,
    w_node_out,
):
    grid_dev, variables = grid_vars.shape
    mesh_dev, width = mesh_latent.shape
    edge_dev = edge_grid.shape[0]
    owners = lax.axis_size("mesh")
    slots = owners * CAP
    rows = edge_dev // LANES
    block = ROWS * LANES
    steps = edge_dev // block
    scale = (edge_dev * lax.axis_size("x") * lax.axis_size("core") * owners) ** (-0.5)
    sds, hbm = jax.ShapeDtypeStruct, pltpu.HBM

    def exchange(value):
        return lax.all_to_all(value, "mesh", 0, 0, tiled=True)

    grid_ids = edge_grid.reshape(rows, LANES)
    slot, ids = call(
        functools.partial(prep_kernel, owners, mesh_dev),
        "prep",
        [sds((rows, LANES), jnp.int32), sds((owners, LANES), jnp.int32)],
        [edge_mesh.reshape(rows, LANES)],
        1e9,
        vmem=60,
    )
    incoming = exchange(ids)

    tile = min(256, grid_dev)
    grid_spec = pl.BlockSpec((tile, width), lambda i: (i, 0))
    hidden, hidden_done = call(
        hidden_kernel,
        "hidden",
        [hbm((grid_dev, width), BF16)],
        [grid_vars, w_in, b_in.reshape(1, width)],
        2 * grid_dev * width * variables,
        grid=(grid_dev // tile,),
        in_specs=[
            pl.BlockSpec((tile, variables), lambda i: (i, 0)),
            whole((variables, width)),
            whole((1, width)),
        ],
        out_specs=[grid_spec],
        after=[ids],
        token=True,
    )

    node_f, node_b = hbm((mesh_dev, width), F32), hbm((mesh_dev, width), BF16)
    self_part, cot_part, node_pre_done = call(
        node_pre_kernel,
        "node_pre",
        [node_f, node_f],
        [mesh_latent, cotangent, w_self, b_node.reshape(1, width), w_node_out],
        4 * mesh_dev * width * width,
        vmem=52,
        after=[hidden_done],
        token=True,
    )
    asked, onehot_in = call(
        ask_kernel,
        "ask",
        [sds((slots, width), BF16), sds((slots, mesh_dev), BF16)],
        [incoming, mesh_latent],
        2 * slots * mesh_dev * width,
        after=[node_pre_done],
    )
    incoming_row = incoming[:, :CAP].reshape(1, slots)
    slot_latent = exchange(asked)

    id_spec = pl.BlockSpec((ROWS, LANES), lambda i: (i, 0))
    edge_spec = pl.BlockSpec((block, width), lambda i: (i, 0))
    edge_t_spec = pl.BlockSpec((width, block), lambda i: (0, i))
    latent_t, edge_pgrid = call(
        grid_kernel,
        "grid",
        [sds((width, grid_dev), BF16), sds((edge_dev, width), BF16)],
        [grid_ids, hidden, w_out, norm_gain.reshape(1, width), u_grid],
        4 * grid_dev * width * width + 2 * edge_dev * grid_dev * width,
        grid=(steps,),
        in_specs=[
            id_spec, whole((grid_dev, width)), whole((width, width)), whole((1, width)),
            whole((width, width)),
        ],
        out_specs=[whole((width, grid_dev)), edge_spec],
        scratch=[pltpu.VMEM((grid_dev, width), BF16)],
        vmem=60,
        after=[asked],
    )

    slots_b, slots_h = sds((slots, width), BF16), hbm((slots, width), BF16)
    slots_spec = whole((slots, width))
    mesh_spec = whole((mesh_dev, width))
    weight_spec = whole((width, width))
    row_spec = whole((1, slots))
    bias = b_edge.reshape(1, width)
    sums, act_sums, slot_pmesh = call(
        functools.partial(edge_kernel, steps),
        "edge",
        [slots_b, slots_h, slots_h],
        [slot, edge_pgrid, slot_latent, u_mesh, bias, w_edge],
        4 * edge_dev * slots * width + 6 * slots * width * width,
        grid=(steps,),
        in_specs=[id_spec, edge_spec, slots_spec, weight_spec, whole((1, width)), weight_spec],
        out_specs=[slots_spec, slots_spec, slots_spec],
        scratch=[pltpu.VMEM((slots, width), F32)],
        vmem=52,
    )
    received = exchange(sums)

    slope, slope_sums, slope_done = call(
        slope_kernel,
        "slope",
        [hbm((edge_dev, width), BF16), hbm((slots, width), F32)],
        [slot, edge_pgrid, slot_pmesh, bias],
        4 * edge_dev * slots * width,
        grid=(steps,),
        in_specs=[id_spec, edge_spec, slots_spec, whole((1, width))],
        out_specs=[edge_spec, slots_spec],
        vmem=60,
        after=[sums],
        token=True,
    )
    g_asked, g_node, node_act = call(
        node_kernel,
        "node",
        [slots_b, node_b, node_b],
        [received, incoming_row, onehot_in, self_part, cot_part, w_agg],
        4 * mesh_dev * width * width + 4 * mesh_dev * slots * width,
        in_specs=[pl.BlockSpec(memory_space=pltpu.VMEM)] * 2 + [pl.BlockSpec(memory_space=pl.ANY)] * 4,
        scratch=[
            pltpu.VMEM((slots, mesh_dev), BF16),
            pltpu.VMEM((mesh_dev, width), F32),
            pltpu.VMEM((mesh_dev, width), F32),
            pltpu.VMEM((width, width), BF16),
            pltpu.SemaphoreType.DMA((4,)),
        ],
        vmem=52,
        after=[slope_done],
    )
    slot_g = exchange(g_asked)

    slots_t_spec = whole((width, slots))
    edge_latent_t, act_sums_t, slot_latent_t, take_done = call(
        take_latent_kernel,
        "take_latent",
        [hbm((width, edge_dev), BF16), hbm((width, slots), BF16), hbm((width, slots), BF16)],
        [grid_ids, latent_t, act_sums, slot_latent],
        2 * edge_dev * grid_dev * width,
        grid=(steps,),
        in_specs=[id_spec, whole((width, grid_dev)), slots_spec, slots_spec],
        out_specs=[edge_t_spec, slots_t_spec, slots_t_spec],
        vmem=52,
        after=[g_asked],
        token=True,
    )
    half = width // 2
    gsum, h = call(
        slot_grad_kernel,
        "slot_grad",
        [slots_h, slots_h],
        [slot_g, w_edge, slope_sums],
        2 * slots * width * width,
        vmem=52,
        after=[take_done],
    )
    gsum_received = exchange(gsum)

    three = hbm((3, half, width), BF16)
    keep, give = call(
        functools.partial(edge_back_kernel, steps),
        "edge_back",
        [three, three],
        [slot, slope, edge_latent_t, h, gsum, slot_latent_t, slot_g, act_sums_t],
        2 * edge_dev * (slots + width) * width + 4 * slots * width * width,
        grid=(steps,),
        in_specs=[id_spec, edge_spec, edge_t_spec, slots_spec] + [pl.BlockSpec(memory_space=pl.ANY)] * 4,
        out_specs=[whole(three.shape), whole(three.shape)],
        scratch=[pltpu.VMEM((width, width), F32)]
        + [pltpu.VMEM(a, BF16) for a in ((slots, width), (width, slots)) * 2]
        + [pltpu.SemaphoreType.DMA((4,))],
        vmem=60,
    )
    others = ("x", "mesh")
    count = lax.axis_size("x") * owners
    pieces = sds((count, 3 * half // count, width), BF16)
    (parts,) = call(
        parts_kernel,
        "parts",
        [pieces],
        [keep, other_core(held(give, [gsum_received]))],
        3 * half * width,
    )
    summed = lax.all_to_all(parts, others, 0, 0, tiled=True)

    mesh_out, grad_mesh, node_post_done = call(
        node_post_kernel,
        "node_post",
        [node_b, node_b],
        [
            gsum_received, incoming_row, g_node, node_act, mesh_latent, cotangent,
            w_node_out, w_self, u_mesh,
        ],
        6 * mesh_dev * width * width + 2 * mesh_dev * slots * width,
        vmem=52,
        after=[parts],
        token=True,
    )
    (copies,) = call(
        functools.partial(spread_kernel, scale),
        "spread",
        [pieces],
        [summed],
        3 * half * width,
        after=[node_post_done],
    )
    mine = lax.all_to_all(copies, others, 0, 0, tiled=True)
    other = other_core(mine)
    grad_ugrid, grad_edge, grad_umesh = finish(False, other, width, finish(True, mine, width))
    return mesh_out, grad_mesh, grad_edge, grad_ugrid, grad_umesh


def solution(mesh):
    bands, owners = mesh.shape["band"], mesh.shape["mesh"]
    cores = 2
    fine = Mesh(mesh.devices.reshape(bands // cores, cores, owners), ("x", "core", "mesh"))
    split = ("x", "core", "mesh")
    return jax.shard_map(
        shards,
        mesh=fine,
        in_specs=(P(split, None),) * 3 + (P(split),) * 2 + (P(),) * 12,
        out_specs=(P(split, None), P(split, None), P(), P(), P()),
        check_vma=False,
    )
```

```python
import functools
import math

import jax
import jax.numpy as jnp
from jax import lax
from jax.experimental import pallas as pl
from jax.experimental.pallas import tpu as pltpu
from jax.sharding import Mesh
from jax.sharding import PartitionSpec as P

CAP = 48
LANES = 128
ROWS = 8
BF16 = jnp.bfloat16
F32 = jnp.float32


def dot(a, b):
    return jnp.dot(a, b, preferred_element_type=F32)


def dot_nt(a, b):
    return lax.dot_general(a, b, (((1,), (1,)), ((), ())), preferred_element_type=F32)


def sigmoid(v):
    return 0.5 + 0.5 * jnp.tanh(0.5 * v)


def as_bf16(mask, one=1.0):
    return jnp.where(mask, one, 0.0).astype(BF16)


def edges_by_ids(ids, count, one=1.0):
    columns = jnp.transpose(ids)
    lanes = lax.broadcasted_iota(jnp.int32, (LANES, count), 1)
    return jnp.concatenate(
        [as_bf16(columns[:, j : j + 1] == lanes, one) for j in range(ids.shape[0])], axis=0
    )


def ids_by_edges(ids, count):
    places = lax.broadcasted_iota(jnp.int32, (count, LANES), 0)
    return jnp.concatenate(
        [as_bf16(ids[j : j + 1, :] == places) for j in range(ids.shape[0])], axis=1
    )


def call(kernel, name, out, args, flops, grid=None, in_specs=None, out_specs=None, scratch=(), vmem=16, after=(), token=False):
    moved = sum(math.prod(a.shape) * a.dtype.itemsize for a in [*args, *out])
    count, last = len(args), len(args) + len(after) + len(out)

    def body(*refs):
        kernel(*refs[:count], *refs[count + len(after) : last], *refs[last + token :])
        if token:
            refs[last][...] = jnp.zeros_like(refs[last])

    if out_specs is None:
        out_specs = [pl.BlockSpec(memory_space=pltpu.VMEM)] * len(out)
    if token:
        out = [*out, jax.ShapeDtypeStruct((8, LANES), jnp.int32)]
        out_specs = [*out_specs, pl.BlockSpec((8, LANES), lambda *_: (0, 0))]
    if in_specs is None:
        in_specs = [pl.BlockSpec(memory_space=pltpu.VMEM)] * count
    extra = {} if grid is None else dict(grid=grid)
    return pl.pallas_call(
        body,
        out_shape=out,
        in_specs=list(in_specs) + [pl.BlockSpec(memory_space=pl.ANY)] * len(after),
        out_specs=out_specs,
        scratch_shapes=scratch,
        name=name,
        cost_estimate=pl.CostEstimate(flops=int(flops), bytes_accessed=int(moved), transcendentals=0),
        compiler_params=pltpu.CompilerParams(vmem_limit_bytes=vmem << 20),
        **extra,
    )(*args, *after)


def whole(shape):
    return pl.BlockSpec(shape, lambda i: (0,) * len(shape))


def band_index():
    return lax.axis_index("x") * lax.axis_size("core") + lax.axis_index("core")


def grid_block(ids_ref, count):
    device = band_index() * lax.axis_size("mesh") + lax.axis_index("mesh")
    return ids_ref[...] - device * count


def prep_kernel(owners, mesh_dev, em_ref, slot_ref, ids_ref):
    m = em_ref[...] - band_index() * (owners * mesh_dev)
    rows = m.shape[0]
    lane = lax.broadcasted_iota(jnp.int32, m.shape, 1)
    row = lax.broadcasted_iota(jnp.int32, m.shape, 0)
    turned = pltpu.roll(m, 1, axis=1)
    before = jnp.where(lane == 0, pltpu.roll(turned, 1, axis=0), turned)
    fresh = (m != before) | ((lane == 0) & (row == 0))
    fresh_b = as_bf16(fresh)
    upto = lax.broadcasted_iota(jnp.int32, (LANES, LANES), 0) <= lax.broadcasted_iota(
        jnp.int32, (LANES, LANES), 1
    )
    inside = dot(fresh_b, as_bf16(upto))
    totals = jnp.broadcast_to(inside[:, LANES - 1 :], inside.shape).astype(BF16)
    above = lax.broadcasted_iota(jnp.int32, (rows, rows), 1) < lax.broadcasted_iota(
        jnp.int32, (rows, rows), 0
    )
    rank = (inside + dot(as_bf16(above), totals)).astype(jnp.int32) - 1
    slot = rank
    local = m
    fresh_i = fresh.astype(jnp.int32)
    for o in range(1, owners):
        past = m >= o * mesh_dev
        start = jnp.sum(
            jnp.sum(jnp.where(past, 0, fresh_i), axis=0, keepdims=True), axis=1, keepdims=True
        )
        slot = jnp.where(past, rank + (o * CAP - start), slot)
        local = jnp.where(past, m - o * mesh_dev, local)
    slot_ref[...] = slot
    value = jnp.where(fresh, local + 1, 0)
    found = []
    for o in range(owners):
        places = o * CAP + lax.broadcasted_iota(jnp.int32, (CAP, LANES), 0)
        total = jnp.zeros((CAP, LANES), jnp.int32)
        for r in range(rows):
            total = total + jnp.where(slot[r : r + 1, :] == places, value[r : r + 1, :], 0)
        found.append(total)
    pad = jnp.zeros((LANES - CAP, LANES), jnp.int32)
    for o in range(owners):
        square = jnp.transpose(jnp.concatenate([found[o], pad], axis=0))
        ids_ref[o : o + 1, :] = jnp.sum(square, axis=0, keepdims=True) - 1


def node_pre_kernel(ml_ref, cot_ref, ws_ref, bn_ref, wno_ref, self_ref, cw_ref):
    self_ref[...] = dot(ml_ref[...], ws_ref[...]) + bn_ref[...]
    cw_ref[...] = dot_nt(cot_ref[...], wno_ref[...])


def hidden_kernel(gv_ref, win_ref, bin_ref, out_ref):
    v = dot(gv_ref[...], win_ref[...]) + bin_ref[...]
    out_ref[...] = (v * sigmoid(v)).astype(BF16)


def grid_kernel(ids_ref, hid_ref, wout_ref, gain_ref, ug_ref, lat_t_ref, out_ref, pg):
    @pl.when(pl.program_id(0) == 0)
    def _():
        out = dot(hid_ref[...], wout_ref[...])
        mean = jnp.mean(out, axis=-1, keepdims=True)
        centred = out - mean
        var = jnp.mean(centred * centred, axis=-1, keepdims=True)
        latent = centred * lax.rsqrt(var + 1e-05) * gain_ref[...]
        pg[...] = dot(latent.astype(BF16), ug_ref[...]).astype(BF16)
        lat_t_ref[...] = jnp.transpose(latent).astype(BF16)

    onehot = edges_by_ids(grid_block(ids_ref, pg.shape[0]), pg.shape[0], 0.5)
    out_ref[...] = dot(onehot, pg[...]).astype(BF16)


def take_latent_kernel(ids_ref, lat_t_ref, act_ref, ml_ref, out_ref, act_t_ref, ml_t_ref):
    @pl.when(pl.program_id(0) == 0)
    def _():
        act_t_ref[...] = jnp.transpose(act_ref[...])
        ml_t_ref[...] = jnp.transpose(ml_ref[...])

    onehot = ids_by_edges(grid_block(ids_ref, lat_t_ref.shape[1]), lat_t_ref.shape[1])
    out_ref[...] = dot(lat_t_ref[...], onehot).astype(BF16)


def ask_kernel(ids_ref, ml_ref, asked_ref, onehot_ref):
    owners = ids_ref.shape[0]
    nodes = ml_ref.shape[0]
    columns = jnp.transpose(ids_ref[...])
    lanes = lax.broadcasted_iota(jnp.int32, (CAP, nodes), 1)
    onehot = jnp.concatenate(
        [as_bf16(columns[:CAP, o : o + 1] == lanes) for o in range(owners)], axis=0
    )
    onehot_ref[...] = onehot
    asked_ref[...] = dot(onehot, ml_ref[...]).astype(BF16)


def half_pre(slot, pm, half_pg, bias):
    return dot(edges_by_ids(slot, pm.shape[0], 0.5), pm) + half_pg.astype(F32) + 0.5 * bias


def edge_kernel(steps, slot_ref, pg_ref, ml_ref, um_ref, be_ref, we_ref, sums_ref, act_ref, pm_ref, total):
    step = pl.program_id(0)

    @pl.when(step == 0)
    def _():
        total[...] = jnp.zeros_like(total)
        pm_ref[...] = dot(ml_ref[...], um_ref[...]).astype(BF16)

    slot = slot_ref[...]
    v = half_pre(slot, pm_ref[...], pg_ref[...], be_ref[...])
    act = (v + v * jnp.tanh(v)).astype(BF16)
    total[...] += dot(ids_by_edges(slot, total.shape[0]), act)

    @pl.when(step == steps - 1)
    def _():
        sums = total[...]
        high = sums.astype(BF16)
        low = (sums - high.astype(F32)).astype(BF16)
        act_ref[...] = high
        sums_ref[...] = (dot(high, we_ref[...]) + dot(low, we_ref[...])).astype(BF16)


def slope_kernel(slot_ref, pg_ref, pm_ref, be_ref, slope_ref, total_ref):
    @pl.when(pl.program_id(0) == 0)
    def _():
        total_ref[...] = jnp.zeros_like(total_ref)

    slot = slot_ref[...]
    v = half_pre(slot, pm_ref[...], pg_ref[...], be_ref[...])
    t = jnp.tanh(v)
    slope = ((1.0 + t) * (1.0 + v * (1.0 - t))).astype(BF16)
    slope_ref[...] = slope
    total_ref[...] += dot(ids_by_edges(slot, total_ref.shape[0]), slope)


def owned(row_ref, rec_ref, nodes):
    places = lax.broadcasted_iota(jnp.int32, (nodes, row_ref.shape[1]), 0)
    return dot(as_bf16(places == row_ref[...]), rec_ref[...]).astype(BF16)


def load(pairs, sems):
    copies = [pltpu.make_async_copy(a, b, sems.at[i]) for i, (a, b) in enumerate(pairs)]
    for copy in copies:
        copy.start()
    return copies


def node_kernel(
    rec_ref, row_ref, oh_hbm, self_hbm, cw_hbm, wa_hbm, gask_ref, gnode_ref, nact_ref,
    oh_ref, self_ref, cw_ref, wa_ref, sems,
):
    pairs = [(wa_hbm, wa_ref), (self_hbm, self_ref), (cw_hbm, cw_ref), (oh_hbm, oh_ref)]
    wa, own, cw, oh = load(pairs, sems)
    agg = owned(row_ref, rec_ref, self_ref.shape[0])
    wa.wait()
    pre = dot(agg, wa_ref[...])
    own.wait()
    pre = self_ref[...] + pre
    s = sigmoid(pre)
    cw.wait()
    g_node = (cw_ref[...] * (s * (1.0 + pre * (1.0 - s)))).astype(BF16)
    g_agg = dot_nt(g_node, wa_ref[...]).astype(BF16)
    oh.wait()
    gask_ref[...] = dot(oh_ref[...], g_agg).astype(BF16)
    gnode_ref[...] = g_node
    nact_ref[...] = (pre * s).astype(BF16)


def slot_grad_kernel(gc_ref, we_ref, slope_ref, gsum_ref, h_ref):
    h = 0.5 * dot_nt(gc_ref[...], we_ref[...])
    h_ref[...] = h.astype(BF16)
    gsum_ref[...] = (h * slope_ref[...]).astype(BF16)


def node_post_kernel(
    rec_ref, row_ref, gnode_ref, nact_ref, ml_ref, cot_ref, wno_ref, ws_ref, um_ref, mo_ref, gm_ref
):
    g_pmesh = owned(row_ref, rec_ref, ml_ref.shape[0])
    mo_ref[...] = (ml_ref[...].astype(F32) + dot(nact_ref[...], wno_ref[...])).astype(BF16)
    gm_ref[...] = (
        cot_ref[...].astype(F32) + dot_nt(gnode_ref[...], ws_ref[...]) + dot_nt(g_pmesh, um_ref[...])
    ).astype(BF16)


def put_halves(place, value, keep_ref, give_ref):
    core = lax.axis_index("core")
    half = value.shape[0] // 2

    @pl.when(core == 0)
    def _():
        keep_ref[place] = value[:half]
        give_ref[place] = value[half:]

    @pl.when(core != 0)
    def _():
        keep_ref[place] = value[half:]
        give_ref[place] = value[:half]


def edge_back_kernel(
    steps, slot_ref, slope_ref, lat_t_ref, h_ref, gsum_hbm, ml_hbm, gc_hbm, act_hbm, keep_ref, give_ref,
    total, gsum_ref, ml_ref, gc_ref, act_ref, sems,
):
    step = pl.program_id(0)
    late = [(act_hbm, act_ref), (gc_hbm, gc_ref), (ml_hbm, ml_ref), (gsum_hbm, gsum_ref)]

    @pl.when(step == 0)
    def _():
        total[...] = jnp.zeros_like(total)
        load(late, sems)

    onehot = edges_by_ids(slot_ref[...], h_ref.shape[0])
    g_edge = (dot(onehot, h_ref[...]) * slope_ref[...].astype(F32)).astype(BF16)
    total[...] += dot(lat_t_ref[...], g_edge)

    @pl.when(step == steps - 1)
    def _():
        for i, (a, b) in enumerate(late):
            pltpu.make_async_copy(a, b, sems.at[i]).wait()
        put_halves(0, total[...].astype(BF16), keep_ref, give_ref)
        put_halves(1, dot(act_ref[...], gc_ref[...]).astype(BF16), keep_ref, give_ref)
        put_halves(2, dot(ml_ref[...], gsum_ref[...]).astype(BF16), keep_ref, give_ref)


def stage_kernel(keep_ref, out_ref):
    out_ref[...] = keep_ref[...]


def parts_kernel(keep_ref, got_ref, out_ref):
    count, _, width = out_ref.shape
    low = keep_ref.shape[1] // count
    for i in range(keep_ref.shape[0]):
        both = (keep_ref[i].astype(F32) + got_ref[i].astype(F32)).astype(BF16)
        out_ref[:, i * low : (i + 1) * low] = both.reshape(count, low, width)


def spread_kernel(scale, parts_ref, out_ref):
    total = (jnp.sum(parts_ref[...].astype(F32), axis=0) * scale).astype(BF16)
    out_ref[...] = jnp.broadcast_to(total[None], out_ref.shape)


def finish_kernel(ours, part_ref, *refs):
    *out_refs, rows_ref, sems = refs[-5:]
    count, rows, width = part_ref.shape
    low = rows // len(out_refs)
    half = count * low
    core = lax.axis_index("core")
    start = pl.multiple_of((core if ours else 1 - core) * half, half)
    copies = []
    for i, out_ref in enumerate(out_refs):
        piece = part_ref[:, i * low : (i + 1) * low]
        rows_ref[i] = piece.astype(F32).reshape(half, width)
        copies.append(pltpu.make_async_copy(rows_ref.at[i], out_ref.at[pl.ds(start, half)], sems.at[i]))
        copies[i].start()
    for copy in copies:
        copy.wait()


def finish(ours, part, width, before=()):
    anywhere = pl.BlockSpec(memory_space=pl.ANY)
    half = width // 2
    return pl.pallas_call(
        functools.partial(finish_kernel, ours),
        out_shape=[jax.ShapeDtypeStruct((width, width), F32)] * 3,
        in_specs=[pl.BlockSpec(memory_space=pltpu.VMEM)] + [anywhere] * len(before),
        out_specs=[anywhere] * 3,
        scratch_shapes=[pltpu.VMEM((3, half, width), F32), pltpu.SemaphoreType.DMA((3,))],
        input_output_aliases={i + 1: i for i in range(len(before))},
        name="finish_ours" if ours else "finish_other",
        cost_estimate=pl.CostEstimate(flops=3 * half * width, bytes_accessed=18 * half * width, transcendentals=0),
        compiler_params=pltpu.CompilerParams(vmem_limit_bytes=16 << 20),
    )(part, *before)


def other_core(value):
    return lax.ppermute(value, "core", [(0, 1), (1, 0)])


def held(value, after):
    def body(*refs):
        pass

    anywhere = pl.BlockSpec(memory_space=pl.ANY)
    return pl.pallas_call(
        body,
        out_shape=jax.ShapeDtypeStruct(value.shape, value.dtype),
        in_specs=[anywhere] * (1 + len(after)),
        out_specs=anywhere,
        input_output_aliases={0: 0},
        name="held",
        compiler_params=pltpu.CompilerParams(vmem_limit_bytes=60 << 20),
    )(value, *after)


def shards(
    grid_vars,
    mesh_latent,
    cotangent,
    edge_grid,
    edge_mesh,
    w_in,
    b_in,
    w_out,
    norm_gain,
    u_grid,
    u_mesh,
    b_edge,
    w_edge,
    w_self,
    w_agg,
    b_node,
    w_node_out,
):
    grid_dev, variables = grid_vars.shape
    mesh_dev, width = mesh_latent.shape
    edge_dev = edge_grid.shape[0]
    owners = lax.axis_size("mesh")
    slots = owners * CAP
    rows = edge_dev // LANES
    block = ROWS * LANES
    steps = edge_dev // block
    scale = (edge_dev * lax.axis_size("x") * lax.axis_size("core") * owners) ** (-0.5)
    sds, hbm = jax.ShapeDtypeStruct, pltpu.HBM

    def exchange(value):
        return lax.all_to_all(value, "mesh", 0, 0, tiled=True)

    grid_ids = edge_grid.reshape(rows, LANES)
    slot, ids = call(
        functools.partial(prep_kernel, owners, mesh_dev),
        "prep",
        [sds((rows, LANES), jnp.int32), sds((owners, LANES), jnp.int32)],
        [edge_mesh.reshape(rows, LANES)],
        1e9,
        vmem=60,
    )
    incoming = exchange(ids)

    tile = min(256, grid_dev)
    grid_spec = pl.BlockSpec((tile, width), lambda i: (i, 0))
    hidden, hidden_done = call(
        hidden_kernel,
        "hidden",
        [hbm((grid_dev, width), BF16)],
        [grid_vars, w_in, b_in.reshape(1, width)],
        2 * grid_dev * width * variables,
        grid=(grid_dev // tile,),
        in_specs=[
            pl.BlockSpec((tile, variables), lambda i: (i, 0)),
            whole((variables, width)),
            whole((1, width)),
        ],
        out_specs=[grid_spec],
        after=[slot],
        token=True,
    )

    node_f, node_b = hbm((mesh_dev, width), F32), hbm((mesh_dev, width), BF16)
    self_part, cot_part, node_pre_done = call(
        node_pre_kernel,
        "node_pre",
        [node_f, node_f],
        [mesh_latent, cotangent, w_self, b_node.reshape(1, width), w_node_out],
        4 * mesh_dev * width * width,
        vmem=52,
        after=[hidden_done],
        token=True,
    )
    asked, onehot_in = call(
        ask_kernel,
        "ask",
        [sds((slots, width), BF16), sds((slots, mesh_dev), BF16)],
        [incoming, mesh_latent],
        2 * slots * mesh_dev * width,
        after=[node_pre_done],
    )
    incoming_row = incoming[:, :CAP].reshape(1, slots)
    slot_latent = exchange(asked)

    id_spec = pl.BlockSpec((ROWS, LANES), lambda i: (i, 0))
    edge_spec = pl.BlockSpec((block, width), lambda i: (i, 0))
    edge_t_spec = pl.BlockSpec((width, block), lambda i: (0, i))
    latent_t, edge_pgrid = call(
        grid_kernel,
        "grid",
        [sds((width, grid_dev), BF16), sds((edge_dev, width), BF16)],
        [grid_ids, hidden, w_out, norm_gain.reshape(1, width), u_grid],
        4 * grid_dev * width * width + 2 * edge_dev * grid_dev * width,
        grid=(steps,),
        in_specs=[
            id_spec, whole((grid_dev, width)), whole((width, width)), whole((1, width)),
            whole((width, width)),
        ],
        out_specs=[whole((width, grid_dev)), edge_spec],
        scratch=[pltpu.VMEM((grid_dev, width), BF16)],
        vmem=60,
        after=[asked],
    )

    slots_b, slots_h = sds((slots, width), BF16), hbm((slots, width), BF16)
    slots_spec = whole((slots, width))
    mesh_spec = whole((mesh_dev, width))
    weight_spec = whole((width, width))
    row_spec = whole((1, slots))
    bias = b_edge.reshape(1, width)
    sums, act_sums, slot_pmesh = call(
        functools.partial(edge_kernel, steps),
        "edge",
        [slots_b, slots_h, slots_h],
        [slot, edge_pgrid, slot_latent, u_mesh, bias, w_edge],
        4 * edge_dev * slots * width + 6 * slots * width * width,
        grid=(steps,),
        in_specs=[id_spec, edge_spec, slots_spec, weight_spec, whole((1, width)), weight_spec],
        out_specs=[slots_spec, slots_spec, slots_spec],
        scratch=[pltpu.VMEM((slots, width), F32)],
        vmem=52,
    )
    received = exchange(sums)

    slope, slope_sums = call(
        slope_kernel,
        "slope",
        [hbm((edge_dev, width), BF16), hbm((slots, width), F32)],
        [slot, edge_pgrid, slot_pmesh, bias],
        4 * edge_dev * slots * width,
        grid=(steps,),
        in_specs=[id_spec, edge_spec, slots_spec, whole((1, width))],
        out_specs=[edge_spec, slots_spec],
        vmem=60,
        after=[sums],
    )
    g_asked, g_node, node_act = call(
        node_kernel,
        "node",
        [slots_b, node_b, node_b],
        [received, incoming_row, onehot_in, self_part, cot_part, w_agg],
        4 * mesh_dev * width * width + 4 * mesh_dev * slots * width,
        in_specs=[pl.BlockSpec(memory_space=pltpu.VMEM)] * 2 + [pl.BlockSpec(memory_space=pl.ANY)] * 4,
        scratch=[
            pltpu.VMEM((slots, mesh_dev), BF16),
            pltpu.VMEM((mesh_dev, width), F32),
            pltpu.VMEM((mesh_dev, width), F32),
            pltpu.VMEM((width, width), BF16),
            pltpu.SemaphoreType.DMA((4,)),
        ],
        vmem=52,
        after=[slope],
    )
    slot_g = exchange(g_asked)

    slots_t_spec = whole((width, slots))
    edge_latent_t, act_sums_t, slot_latent_t, take_done = call(
        take_latent_kernel,
        "take_latent",
        [hbm((width, edge_dev), BF16), hbm((width, slots), BF16), hbm((width, slots), BF16)],
        [grid_ids, latent_t, act_sums, slot_latent],
        2 * edge_dev * grid_dev * width,
        grid=(steps,),
        in_specs=[id_spec, whole((width, grid_dev)), slots_spec, slots_spec],
        out_specs=[edge_t_spec, slots_t_spec, slots_t_spec],
        vmem=52,
        after=[g_asked],
        token=True,
    )
    half = width // 2
    gsum, h = call(
        slot_grad_kernel,
        "slot_grad",
        [slots_h, slots_h],
        [slot_g, w_edge, slope_sums],
        2 * slots * width * width,
        vmem=52,
        after=[take_done],
    )
    gsum_received = exchange(gsum)

    three = hbm((3, half, width), BF16)
    keep, give = call(
        functools.partial(edge_back_kernel, steps),
        "edge_back",
        [three, three],
        [slot, slope, edge_latent_t, h, gsum, slot_latent_t, slot_g, act_sums_t],
        2 * edge_dev * (slots + width) * width + 4 * slots * width * width,
        grid=(steps,),
        in_specs=[id_spec, edge_spec, edge_t_spec, slots_spec] + [pl.BlockSpec(memory_space=pl.ANY)] * 4,
        out_specs=[whole(three.shape), whole(three.shape)],
        scratch=[pltpu.VMEM((width, width), F32)]
        + [pltpu.VMEM(a, BF16) for a in ((slots, width), (width, slots)) * 2]
        + [pltpu.SemaphoreType.DMA((4,))],
        vmem=60,
    )
    others = ("x", "mesh")
    count = lax.axis_size("x") * owners
    pieces = sds((count, 3 * half // count, width), BF16)
    (staged,) = call(stage_kernel, "stage", [sds((3, half, width), BF16)], [keep], half * width)
    (parts,) = call(
        parts_kernel,
        "parts",
        [pieces],
        [staged, other_core(held(give, [gsum_received]))],
        3 * half * width,
    )
    summed = lax.all_to_all(parts, others, 0, 0, tiled=True)

    mesh_out, grad_mesh, node_post_done = call(
        node_post_kernel,
        "node_post",
        [node_b, node_b],
        [
            gsum_received, incoming_row, g_node, node_act, mesh_latent, cotangent,
            w_node_out, w_self, u_mesh,
        ],
        6 * mesh_dev * width * width + 2 * mesh_dev * slots * width,
        vmem=52,
        after=[parts],
        token=True,
    )
    (copies,) = call(
        functools.partial(spread_kernel, scale),
        "spread",
        [pieces],
        [summed],
        3 * half * width,
        after=[node_post_done],
    )
    mine = lax.all_to_all(copies, others, 0, 0, tiled=True)
    other = other_core(mine)
    grad_ugrid, grad_edge, grad_umesh = finish(False, other, width, finish(True, mine, width))
    return mesh_out, grad_mesh, grad_edge, grad_ugrid, grad_umesh


def solution(mesh):
    bands, owners = mesh.shape["band"], mesh.shape["mesh"]
    cores = 2
    fine = Mesh(mesh.devices.reshape(bands // cores, cores, owners), ("x", "core", "mesh"))
    split = ("x", "core", "mesh")
    return jax.shard_map(
        shards,
        mesh=fine,
        in_specs=(P(split, None),) * 3 + (P(split),) * 2 + (P(),) * 12,
        out_specs=(P(split, None), P(split, None), P(), P(), P()),
        check_vma=False,
    )
```

```python
import functools
import math

import jax
import jax.numpy as jnp
from jax import lax
from jax.experimental import pallas as pl
from jax.experimental.pallas import tpu as pltpu
from jax.sharding import Mesh
from jax.sharding import PartitionSpec as P

CAP = 48
LANES = 128
ROWS = 8
BF16 = jnp.bfloat16
F32 = jnp.float32


def dot(a, b):
    return jnp.dot(a, b, preferred_element_type=F32)


def dot_nt(a, b):
    return lax.dot_general(a, b, (((1,), (1,)), ((), ())), preferred_element_type=F32)


def sigmoid(v):
    return 0.5 + 0.5 * jnp.tanh(0.5 * v)


def as_bf16(mask, one=1.0):
    return jnp.where(mask, one, 0.0).astype(BF16)


def edges_by_ids(ids, count, one=1.0):
    columns = jnp.transpose(ids)
    lanes = lax.broadcasted_iota(jnp.int32, (LANES, count), 1)
    return jnp.concatenate(
        [as_bf16(columns[:, j : j + 1] == lanes, one) for j in range(ids.shape[0])], axis=0
    )


def ids_by_edges(ids, count):
    places = lax.broadcasted_iota(jnp.int32, (count, LANES), 0)
    return jnp.concatenate(
        [as_bf16(ids[j : j + 1, :] == places) for j in range(ids.shape[0])], axis=1
    )


def call(kernel, name, out, args, flops, grid=None, in_specs=None, out_specs=None, scratch=(), vmem=16, after=(), token=False):
    moved = sum(math.prod(a.shape) * a.dtype.itemsize for a in [*args, *out])
    count, last = len(args), len(args) + len(after) + len(out)

    def body(*refs):
        kernel(*refs[:count], *refs[count + len(after) : last], *refs[last + token :])
        if token:
            refs[last][...] = jnp.zeros_like(refs[last])

    if out_specs is None:
        out_specs = [pl.BlockSpec(memory_space=pltpu.VMEM)] * len(out)
    if token:
        out = [*out, jax.ShapeDtypeStruct((8, LANES), jnp.int32)]
        out_specs = [*out_specs, pl.BlockSpec((8, LANES), lambda *_: (0, 0))]
    if in_specs is None:
        in_specs = [pl.BlockSpec(memory_space=pltpu.VMEM)] * count
    extra = {} if grid is None else dict(grid=grid)
    return pl.pallas_call(
        body,
        out_shape=out,
        in_specs=list(in_specs) + [pl.BlockSpec(memory_space=pl.ANY)] * len(after),
        out_specs=out_specs,
        scratch_shapes=scratch,
        name=name,
        cost_estimate=pl.CostEstimate(flops=int(flops), bytes_accessed=int(moved), transcendentals=0),
        compiler_params=pltpu.CompilerParams(vmem_limit_bytes=vmem << 20),
        **extra,
    )(*args, *after)


def whole(shape):
    return pl.BlockSpec(shape, lambda i: (0,) * len(shape))


def band_index():
    return lax.axis_index("x") * lax.axis_size("core") + lax.axis_index("core")


def grid_block(ids_ref, count):
    device = band_index() * lax.axis_size("mesh") + lax.axis_index("mesh")
    return ids_ref[...] - device * count


def prep_kernel(owners, mesh_dev, em_ref, slot_ref, ids_ref):
    m = em_ref[...] - band_index() * (owners * mesh_dev)
    rows = m.shape[0]
    lane = lax.broadcasted_iota(jnp.int32, m.shape, 1)
    row = lax.broadcasted_iota(jnp.int32, m.shape, 0)
    turned = pltpu.roll(m, 1, axis=1)
    before = jnp.where(lane == 0, pltpu.roll(turned, 1, axis=0), turned)
    fresh = (m != before) | ((lane == 0) & (row == 0))
    fresh_b = as_bf16(fresh)
    upto = lax.broadcasted_iota(jnp.int32, (LANES, LANES), 0) <= lax.broadcasted_iota(
        jnp.int32, (LANES, LANES), 1
    )
    inside = dot(fresh_b, as_bf16(upto))
    totals = jnp.broadcast_to(inside[:, LANES - 1 :], inside.shape).astype(BF16)
    above = lax.broadcasted_iota(jnp.int32, (rows, rows), 1) < lax.broadcasted_iota(
        jnp.int32, (rows, rows), 0
    )
    rank = (inside + dot(as_bf16(above), totals)).astype(jnp.int32) - 1
    slot = rank
    local = m
    fresh_i = fresh.astype(jnp.int32)
    for o in range(1, owners):
        past = m >= o * mesh_dev
        start = jnp.sum(
            jnp.sum(jnp.where(past, 0, fresh_i), axis=0, keepdims=True), axis=1, keepdims=True
        )
        slot = jnp.where(past, rank + (o * CAP - start), slot)
        local = jnp.where(past, m - o * mesh_dev, local)
    slot_ref[...] = slot
    value = jnp.where(fresh, local + 1, 0)
    found = []
    for o in range(owners):
        places = o * CAP + lax.broadcasted_iota(jnp.int32, (CAP, LANES), 0)
        total = jnp.zeros((CAP, LANES), jnp.int32)
        for r in range(rows):
            total = total + jnp.where(slot[r : r + 1, :] == places, value[r : r + 1, :], 0)
        found.append(total)
    pad = jnp.zeros((LANES - CAP, LANES), jnp.int32)
    for o in range(owners):
        square = jnp.transpose(jnp.concatenate([found[o], pad], axis=0))
        ids_ref[o : o + 1, :] = jnp.sum(square, axis=0, keepdims=True) - 1


def node_pre_kernel(ml_ref, cot_ref, ws_ref, bn_ref, wno_ref, self_ref, cw_ref):
    self_ref[...] = dot(ml_ref[...], ws_ref[...]) + bn_ref[...]
    cw_ref[...] = dot_nt(cot_ref[...], wno_ref[...])


def hidden_kernel(gv_ref, win_ref, bin_ref, out_ref):
    v = dot(gv_ref[...], win_ref[...]) + bin_ref[...]
    out_ref[...] = (v * sigmoid(v)).astype(BF16)


def grid_kernel(ids_ref, hid_ref, wout_ref, gain_ref, ug_ref, lat_t_ref, out_ref, pg):
    @pl.when(pl.program_id(0) == 0)
    def _():
        out = dot(hid_ref[...], wout_ref[...])
        mean = jnp.mean(out, axis=-1, keepdims=True)
        centred = out - mean
        var = jnp.mean(centred * centred, axis=-1, keepdims=True)
        latent = centred * lax.rsqrt(var + 1e-05) * gain_ref[...]
        pg[...] = dot(latent.astype(BF16), ug_ref[...]).astype(BF16)
        lat_t_ref[...] = jnp.transpose(latent).astype(BF16)

    onehot = edges_by_ids(grid_block(ids_ref, pg.shape[0]), pg.shape[0], 0.5)
    out_ref[...] = dot(onehot, pg[...]).astype(BF16)


def take_latent_kernel(ids_ref, lat_t_ref, act_ref, ml_ref, out_ref, act_t_ref, ml_t_ref):
    @pl.when(pl.program_id(0) == 0)
    def _():
        act_t_ref[...] = jnp.transpose(act_ref[...])
        ml_t_ref[...] = jnp.transpose(ml_ref[...])

    onehot = ids_by_edges(grid_block(ids_ref, lat_t_ref.shape[1]), lat_t_ref.shape[1])
    out_ref[...] = dot(lat_t_ref[...], onehot).astype(BF16)


def ask_kernel(ids_ref, ml_ref, asked_ref, onehot_ref):
    owners = ids_ref.shape[0]
    nodes = ml_ref.shape[0]
    columns = jnp.transpose(ids_ref[...])
    lanes = lax.broadcasted_iota(jnp.int32, (CAP, nodes), 1)
    onehot = jnp.concatenate(
        [as_bf16(columns[:CAP, o : o + 1] == lanes) for o in range(owners)], axis=0
    )
    onehot_ref[...] = onehot
    asked_ref[...] = dot(onehot, ml_ref[...]).astype(BF16)


def half_pre(slot, pm, half_pg, bias):
    return dot(edges_by_ids(slot, pm.shape[0], 0.5), pm) + half_pg.astype(F32) + 0.5 * bias


def edge_kernel(steps, slot_ref, pg_ref, ml_ref, um_ref, be_ref, we_ref, sums_ref, act_ref, pm_ref, total):
    step = pl.program_id(0)

    @pl.when(step == 0)
    def _():
        total[...] = jnp.zeros_like(total)
        pm_ref[...] = dot(ml_ref[...], um_ref[...]).astype(BF16)

    slot = slot_ref[...]
    v = half_pre(slot, pm_ref[...], pg_ref[...], be_ref[...])
    act = (v + v * jnp.tanh(v)).astype(BF16)
    total[...] += dot(ids_by_edges(slot, total.shape[0]), act)

    @pl.when(step == steps - 1)
    def _():
        sums = total[...]
        high = sums.astype(BF16)
        low = (sums - high.astype(F32)).astype(BF16)
        act_ref[...] = high
        sums_ref[...] = (dot(high, we_ref[...]) + dot(low, we_ref[...])).astype(BF16)


def slope_kernel(slot_ref, pg_ref, pm_ref, be_ref, slope_ref, total_ref):
    @pl.when(pl.program_id(0) == 0)
    def _():
        total_ref[...] = jnp.zeros_like(total_ref)

    slot = slot_ref[...]
    v = half_pre(slot, pm_ref[...], pg_ref[...], be_ref[...])
    t = jnp.tanh(v)
    slope = ((1.0 + t) * (1.0 + v * (1.0 - t))).astype(BF16)
    slope_ref[...] = slope
    total_ref[...] += dot(ids_by_edges(slot, total_ref.shape[0]), slope)


def owned(row_ref, rec_ref, nodes):
    places = lax.broadcasted_iota(jnp.int32, (nodes, row_ref.shape[1]), 0)
    return dot(as_bf16(places == row_ref[...]), rec_ref[...]).astype(BF16)


def load(pairs, sems):
    copies = [pltpu.make_async_copy(a, b, sems.at[i]) for i, (a, b) in enumerate(pairs)]
    for copy in copies:
        copy.start()
    return copies


def node_kernel(
    rec_ref, row_ref, oh_hbm, self_hbm, cw_hbm, wa_hbm, gask_ref, gnode_ref, nact_ref,
    oh_ref, self_ref, cw_ref, wa_ref, sems,
):
    pairs = [(wa_hbm, wa_ref), (self_hbm, self_ref), (cw_hbm, cw_ref), (oh_hbm, oh_ref)]
    wa, own, cw, oh = load(pairs, sems)
    agg = owned(row_ref, rec_ref, self_ref.shape[0])
    wa.wait()
    pre = dot(agg, wa_ref[...])
    own.wait()
    pre = self_ref[...] + pre
    s = sigmoid(pre)
    cw.wait()
    g_node = (cw_ref[...] * (s * (1.0 + pre * (1.0 - s)))).astype(BF16)
    g_agg = dot_nt(g_node, wa_ref[...]).astype(BF16)
    oh.wait()
    gask_ref[...] = dot(oh_ref[...], g_agg).astype(BF16)
    gnode_ref[...] = g_node
    nact_ref[...] = (pre * s).astype(BF16)


def slot_grad_kernel(gc_ref, we_ref, slope_ref, gsum_ref, h_ref):
    h = 0.5 * dot_nt(gc_ref[...], we_ref[...])
    h_ref[...] = h.astype(BF16)
    gsum_ref[...] = (h * slope_ref[...]).astype(BF16)


def node_post_kernel(
    rec_ref, row_ref, gnode_ref, nact_ref, ml_ref, cot_ref, wno_ref, ws_ref, um_ref, mo_ref, gm_ref
):
    g_pmesh = owned(row_ref, rec_ref, ml_ref.shape[0])
    mo_ref[...] = (ml_ref[...].astype(F32) + dot(nact_ref[...], wno_ref[...])).astype(BF16)
    gm_ref[...] = (
        cot_ref[...].astype(F32) + dot_nt(gnode_ref[...], ws_ref[...]) + dot_nt(g_pmesh, um_ref[...])
    ).astype(BF16)


def put_halves(place, value, keep_ref, give_ref):
    core = lax.axis_index("core")
    half = value.shape[0] // 2

    @pl.when(core == 0)
    def _():
        keep_ref[place] = value[:half]
        give_ref[place] = value[half:]

    @pl.when(core != 0)
    def _():
        keep_ref[place] = value[half:]
        give_ref[place] = value[:half]


def edge_back_kernel(
    steps, slot_ref, slope_ref, lat_t_ref, h_ref, gsum_hbm, ml_hbm, gc_hbm, act_hbm, keep_hbm, give_hbm,
    total, gsum_ref, ml_ref, gc_ref, act_ref, keep_ref, give_ref, sems, out_sems,
):
    step = pl.program_id(0)
    late = [(act_hbm, act_ref), (gc_hbm, gc_ref), (ml_hbm, ml_ref), (gsum_hbm, gsum_ref)]

    def leaving(which):
        rows = pl.ds(1, 2) if which else pl.ds(0, 1)
        return [
            pltpu.make_async_copy(keep_ref.at[rows], keep_hbm.at[rows], out_sems.at[2 * which]),
            pltpu.make_async_copy(give_ref.at[rows], give_hbm.at[rows], out_sems.at[2 * which + 1]),
        ]

    @pl.when(step == 0)
    def _():
        total[...] = jnp.zeros_like(total)
        load(late, sems)

    onehot = edges_by_ids(slot_ref[...], h_ref.shape[0])
    g_edge = (dot(onehot, h_ref[...]) * slope_ref[...].astype(F32)).astype(BF16)
    total[...] += dot(lat_t_ref[...], g_edge)

    @pl.when(step == max(steps - 2, 0))
    def _():
        for i, (a, b) in enumerate(late):
            pltpu.make_async_copy(a, b, sems.at[i]).wait()
        put_halves(1, dot(act_ref[...], gc_ref[...]).astype(BF16), keep_ref, give_ref)
        put_halves(2, dot(ml_ref[...], gsum_ref[...]).astype(BF16), keep_ref, give_ref)
        for copy in leaving(1):
            copy.start()

    @pl.when(step == steps - 1)
    def _():
        put_halves(0, total[...].astype(BF16), keep_ref, give_ref)
        for copy in leaving(0):
            copy.start()
        for copy in leaving(1) + leaving(0):
            copy.wait()


def stage_kernel(keep_ref, out_ref):
    out_ref[...] = keep_ref[...]


def parts_kernel(keep_ref, got_ref, out_ref):
    count, _, width = out_ref.shape
    low = keep_ref.shape[1] // count
    for i in range(keep_ref.shape[0]):
        both = (keep_ref[i].astype(F32) + got_ref[i].astype(F32)).astype(BF16)
        out_ref[:, i * low : (i + 1) * low] = both.reshape(count, low, width)


def spread_kernel(scale, parts_ref, out_ref):
    total = (jnp.sum(parts_ref[...].astype(F32), axis=0) * scale).astype(BF16)
    out_ref[...] = jnp.broadcast_to(total[None], out_ref.shape)


def finish_kernel(ours, part_ref, *refs):
    *out_refs, rows_ref, sems = refs[-5:]
    count, rows, width = part_ref.shape
    low = rows // len(out_refs)
    half = count * low
    core = lax.axis_index("core")
    start = pl.multiple_of((core if ours else 1 - core) * half, half)
    copies = []
    for i, out_ref in enumerate(out_refs):
        piece = part_ref[:, i * low : (i + 1) * low]
        rows_ref[i] = piece.astype(F32).reshape(half, width)
        copies.append(pltpu.make_async_copy(rows_ref.at[i], out_ref.at[pl.ds(start, half)], sems.at[i]))
        copies[i].start()
    for copy in copies:
        copy.wait()


def finish(ours, part, width, before=()):
    anywhere = pl.BlockSpec(memory_space=pl.ANY)
    half = width // 2
    return pl.pallas_call(
        functools.partial(finish_kernel, ours),
        out_shape=[jax.ShapeDtypeStruct((width, width), F32)] * 3,
        in_specs=[pl.BlockSpec(memory_space=pltpu.VMEM)] + [anywhere] * len(before),
        out_specs=[anywhere] * 3,
        scratch_shapes=[pltpu.VMEM((3, half, width), F32), pltpu.SemaphoreType.DMA((3,))],
        input_output_aliases={i + 1: i for i in range(len(before))},
        name="finish_ours" if ours else "finish_other",
        cost_estimate=pl.CostEstimate(flops=3 * half * width, bytes_accessed=18 * half * width, transcendentals=0),
        compiler_params=pltpu.CompilerParams(vmem_limit_bytes=16 << 20),
    )(part, *before)


def other_core(value):
    return lax.ppermute(value, "core", [(0, 1), (1, 0)])


def held(value, after):
    def body(*refs):
        pass

    anywhere = pl.BlockSpec(memory_space=pl.ANY)
    return pl.pallas_call(
        body,
        out_shape=jax.ShapeDtypeStruct(value.shape, value.dtype),
        in_specs=[anywhere] * (1 + len(after)),
        out_specs=anywhere,
        input_output_aliases={0: 0},
        name="held",
        compiler_params=pltpu.CompilerParams(vmem_limit_bytes=60 << 20),
    )(value, *after)


def shards(
    grid_vars,
    mesh_latent,
    cotangent,
    edge_grid,
    edge_mesh,
    w_in,
    b_in,
    w_out,
    norm_gain,
    u_grid,
    u_mesh,
    b_edge,
    w_edge,
    w_self,
    w_agg,
    b_node,
    w_node_out,
):
    grid_dev, variables = grid_vars.shape
    mesh_dev, width = mesh_latent.shape
    edge_dev = edge_grid.shape[0]
    owners = lax.axis_size("mesh")
    slots = owners * CAP
    rows = edge_dev // LANES
    block = ROWS * LANES
    steps = edge_dev // block
    scale = (edge_dev * lax.axis_size("x") * lax.axis_size("core") * owners) ** (-0.5)
    sds, hbm = jax.ShapeDtypeStruct, pltpu.HBM

    def exchange(value):
        return lax.all_to_all(value, "mesh", 0, 0, tiled=True)

    grid_ids = edge_grid.reshape(rows, LANES)
    slot, ids = call(
        functools.partial(prep_kernel, owners, mesh_dev),
        "prep",
        [sds((rows, LANES), jnp.int32), sds((owners, LANES), jnp.int32)],
        [edge_mesh.reshape(rows, LANES)],
        1e9,
        vmem=60,
    )
    incoming = exchange(ids)

    tile = min(256, grid_dev)
    grid_spec = pl.BlockSpec((tile, width), lambda i: (i, 0))
    hidden, hidden_done = call(
        hidden_kernel,
        "hidden",
        [hbm((grid_dev, width), BF16)],
        [grid_vars, w_in, b_in.reshape(1, width)],
        2 * grid_dev * width * variables,
        grid=(grid_dev // tile,),
        in_specs=[
            pl.BlockSpec((tile, variables), lambda i: (i, 0)),
            whole((variables, width)),
            whole((1, width)),
        ],
        out_specs=[grid_spec],
        after=[slot],
        token=True,
    )

    node_f, node_b = hbm((mesh_dev, width), F32), hbm((mesh_dev, width), BF16)
    self_part, cot_part, node_pre_done = call(
        node_pre_kernel,
        "node_pre",
        [node_f, node_f],
        [mesh_latent, cotangent, w_self, b_node.reshape(1, width), w_node_out],
        4 * mesh_dev * width * width,
        vmem=52,
        after=[hidden_done],
        token=True,
    )
    asked, onehot_in = call(
        ask_kernel,
        "ask",
        [sds((slots, width), BF16), sds((slots, mesh_dev), BF16)],
        [incoming, mesh_latent],
        2 * slots * mesh_dev * width,
        after=[node_pre_done],
    )
    incoming_row = incoming[:, :CAP].reshape(1, slots)
    slot_latent = exchange(asked)

    id_spec = pl.BlockSpec((ROWS, LANES), lambda i: (i, 0))
    edge_spec = pl.BlockSpec((block, width), lambda i: (i, 0))
    edge_t_spec = pl.BlockSpec((width, block), lambda i: (0, i))
    latent_t, edge_pgrid = call(
        grid_kernel,
        "grid",
        [sds((width, grid_dev), BF16), sds((edge_dev, width), BF16)],
        [grid_ids, hidden, w_out, norm_gain.reshape(1, width), u_grid],
        4 * grid_dev * width * width + 2 * edge_dev * grid_dev * width,
        grid=(steps,),
        in_specs=[
            id_spec, whole((grid_dev, width)), whole((width, width)), whole((1, width)),
            whole((width, width)),
        ],
        out_specs=[whole((width, grid_dev)), edge_spec],
        scratch=[pltpu.VMEM((grid_dev, width), BF16)],
        vmem=60,
        after=[asked],
    )

    slots_b, slots_h = sds((slots, width), BF16), hbm((slots, width), BF16)
    slots_spec = whole((slots, width))
    mesh_spec = whole((mesh_dev, width))
    weight_spec = whole((width, width))
    row_spec = whole((1, slots))
    bias = b_edge.reshape(1, width)
    sums, act_sums, slot_pmesh = call(
        functools.partial(edge_kernel, steps),
        "edge",
        [slots_b, slots_h, slots_h],
        [slot, edge_pgrid, slot_latent, u_mesh, bias, w_edge],
        4 * edge_dev * slots * width + 6 * slots * width * width,
        grid=(steps,),
        in_specs=[id_spec, edge_spec, slots_spec, weight_spec, whole((1, width)), weight_spec],
        out_specs=[slots_spec, slots_spec, slots_spec],
        scratch=[pltpu.VMEM((slots, width), F32)],
        vmem=52,
    )
    received = exchange(sums)

    slope, slope_sums = call(
        slope_kernel,
        "slope",
        [hbm((edge_dev, width), BF16), hbm((slots, width), F32)],
        [slot, edge_pgrid, slot_pmesh, bias],
        4 * edge_dev * slots * width,
        grid=(steps,),
        in_specs=[id_spec, edge_spec, slots_spec, whole((1, width))],
        out_specs=[edge_spec, slots_spec],
        vmem=60,
        after=[sums],
    )
    g_asked, g_node, node_act = call(
        node_kernel,
        "node",
        [slots_b, node_b, node_b],
        [received, incoming_row, onehot_in, self_part, cot_part, w_agg],
        4 * mesh_dev * width * width + 4 * mesh_dev * slots * width,
        in_specs=[pl.BlockSpec(memory_space=pltpu.VMEM)] * 2 + [pl.BlockSpec(memory_space=pl.ANY)] * 4,
        scratch=[
            pltpu.VMEM((slots, mesh_dev), BF16),
            pltpu.VMEM((mesh_dev, width), F32),
            pltpu.VMEM((mesh_dev, width), F32),
            pltpu.VMEM((width, width), BF16),
            pltpu.SemaphoreType.DMA((4,)),
        ],
        vmem=52,
        after=[slope],
    )
    slot_g = exchange(g_asked)

    slots_t_spec = whole((width, slots))
    edge_latent_t, act_sums_t, slot_latent_t, take_done = call(
        take_latent_kernel,
        "take_latent",
        [hbm((width, edge_dev), BF16), hbm((width, slots), BF16), hbm((width, slots), BF16)],
        [grid_ids, latent_t, act_sums, slot_latent],
        2 * edge_dev * grid_dev * width,
        grid=(steps,),
        in_specs=[id_spec, whole((width, grid_dev)), slots_spec, slots_spec],
        out_specs=[edge_t_spec, slots_t_spec, slots_t_spec],
        vmem=52,
        after=[g_asked],
        token=True,
    )
    half = width // 2
    gsum, h = call(
        slot_grad_kernel,
        "slot_grad",
        [slots_h, slots_h],
        [slot_g, w_edge, slope_sums],
        2 * slots * width * width,
        vmem=52,
        after=[take_done],
    )
    gsum_received = exchange(gsum)

    three = hbm((3, half, width), BF16)
    keep, give = call(
        functools.partial(edge_back_kernel, steps),
        "edge_back",
        [three, three],
        [slot, slope, edge_latent_t, h, gsum, slot_latent_t, slot_g, act_sums_t],
        2 * edge_dev * (slots + width) * width + 4 * slots * width * width,
        grid=(steps,),
        in_specs=[id_spec, edge_spec, edge_t_spec, slots_spec] + [pl.BlockSpec(memory_space=pl.ANY)] * 4,
        out_specs=[pl.BlockSpec(memory_space=pl.ANY)] * 2,
        scratch=[pltpu.VMEM((width, width), F32)]
        + [pltpu.VMEM(a, BF16) for a in ((slots, width), (width, slots)) * 2]
        + [pltpu.VMEM((3, half, width), BF16)] * 2
        + [pltpu.SemaphoreType.DMA((4,))] * 2,
        vmem=60,
    )
    others = ("x", "mesh")
    count = lax.axis_size("x") * owners
    pieces = sds((count, 3 * half // count, width), BF16)
    (staged,) = call(stage_kernel, "stage", [sds((3, half, width), BF16)], [keep], half * width)
    (parts,) = call(
        parts_kernel,
        "parts",
        [pieces],
        [staged, other_core(held(give, [gsum_received]))],
        3 * half * width,
    )
    summed = lax.all_to_all(parts, others, 0, 0, tiled=True)

    mesh_out, grad_mesh, node_post_done = call(
        node_post_kernel,
        "node_post",
        [node_b, node_b],
        [
            gsum_received, incoming_row, g_node, node_act, mesh_latent, cotangent,
            w_node_out, w_self, u_mesh,
        ],
        6 * mesh_dev * width * width + 2 * mesh_dev * slots * width,
        vmem=52,
        after=[parts],
        token=True,
    )
    (copies,) = call(
        functools.partial(spread_kernel, scale),
        "spread",
        [pieces],
        [summed],
        3 * half * width,
        after=[node_post_done],
    )
    mine = lax.all_to_all(copies, others, 0, 0, tiled=True)
    other = other_core(mine)
    grad_ugrid, grad_edge, grad_umesh = finish(False, other, width, finish(True, mine, width))
    return mesh_out, grad_mesh, grad_edge, grad_ugrid, grad_umesh


def solution(mesh):
    bands, owners = mesh.shape["band"], mesh.shape["mesh"]
    cores = 2
    fine = Mesh(mesh.devices.reshape(bands // cores, cores, owners), ("x", "core", "mesh"))
    split = ("x", "core", "mesh")
    return jax.shard_map(
        shards,
        mesh=fine,
        in_specs=(P(split, None),) * 3 + (P(split),) * 2 + (P(),) * 12,
        out_specs=(P(split, None), P(split, None), P(), P(), P()),
        check_vma=False,
    )
```

```python
import functools
import math

import jax
import jax.numpy as jnp
from jax import lax
from jax.experimental import pallas as pl
from jax.experimental.pallas import tpu as pltpu
from jax.sharding import Mesh
from jax.sharding import PartitionSpec as P

CAP = 48
LANES = 128
ROWS = 8
BF16 = jnp.bfloat16
F32 = jnp.float32


def dot(a, b):
    return jnp.dot(a, b, preferred_element_type=F32)


def dot_nt(a, b):
    return lax.dot_general(a, b, (((1,), (1,)), ((), ())), preferred_element_type=F32)


def sigmoid(v):
    return 0.5 + 0.5 * jnp.tanh(0.5 * v)


def as_bf16(mask, one=1.0):
    return jnp.where(mask, one, 0.0).astype(BF16)


def edges_by_ids(ids, count, one=1.0):
    columns = jnp.transpose(ids)
    lanes = lax.broadcasted_iota(jnp.int32, (LANES, count), 1)
    return jnp.concatenate(
        [as_bf16(columns[:, j : j + 1] == lanes, one) for j in range(ids.shape[0])], axis=0
    )


def ids_by_edges(ids, count):
    places = lax.broadcasted_iota(jnp.int32, (count, LANES), 0)
    return jnp.concatenate(
        [as_bf16(ids[j : j + 1, :] == places) for j in range(ids.shape[0])], axis=1
    )


def call(kernel, name, out, args, flops, grid=None, in_specs=None, out_specs=None, scratch=(), vmem=16, after=(), token=False):
    moved = sum(math.prod(a.shape) * a.dtype.itemsize for a in [*args, *out])
    count, last = len(args), len(args) + len(after) + len(out)

    def body(*refs):
        kernel(*refs[:count], *refs[count + len(after) : last], *refs[last + token :])
        if token:
            refs[last][...] = jnp.zeros_like(refs[last])

    if out_specs is None:
        out_specs = [pl.BlockSpec(memory_space=pltpu.VMEM)] * len(out)
    if token:
        out = [*out, jax.ShapeDtypeStruct((8, LANES), jnp.int32)]
        out_specs = [*out_specs, pl.BlockSpec((8, LANES), lambda *_: (0, 0))]
    if in_specs is None:
        in_specs = [pl.BlockSpec(memory_space=pltpu.VMEM)] * count
    extra = {} if grid is None else dict(grid=grid)
    return pl.pallas_call(
        body,
        out_shape=out,
        in_specs=list(in_specs) + [pl.BlockSpec(memory_space=pl.ANY)] * len(after),
        out_specs=out_specs,
        scratch_shapes=scratch,
        name=name,
        cost_estimate=pl.CostEstimate(flops=int(flops), bytes_accessed=int(moved), transcendentals=0),
        compiler_params=pltpu.CompilerParams(vmem_limit_bytes=vmem << 20),
        **extra,
    )(*args, *after)


def whole(shape):
    return pl.BlockSpec(shape, lambda i: (0,) * len(shape))


def band_index():
    return lax.axis_index("x") * lax.axis_size("core") + lax.axis_index("core")


def grid_block(ids_ref, count):
    device = band_index() * lax.axis_size("mesh") + lax.axis_index("mesh")
    return ids_ref[...] - device * count


def prep_kernel(owners, mesh_dev, em_ref, slot_ref, ids_ref):
    m = em_ref[...] - band_index() * (owners * mesh_dev)
    rows = m.shape[0]
    lane = lax.broadcasted_iota(jnp.int32, m.shape, 1)
    row = lax.broadcasted_iota(jnp.int32, m.shape, 0)
    turned = pltpu.roll(m, 1, axis=1)
    before = jnp.where(lane == 0, pltpu.roll(turned, 1, axis=0), turned)
    fresh = (m != before) | ((lane == 0) & (row == 0))
    fresh_b = as_bf16(fresh)
    upto = lax.broadcasted_iota(jnp.int32, (LANES, LANES), 0) <= lax.broadcasted_iota(
        jnp.int32, (LANES, LANES), 1
    )
    inside = dot(fresh_b, as_bf16(upto))
    totals = jnp.broadcast_to(inside[:, LANES - 1 :], inside.shape).astype(BF16)
    above = lax.broadcasted_iota(jnp.int32, (rows, rows), 1) < lax.broadcasted_iota(
        jnp.int32, (rows, rows), 0
    )
    rank = (inside + dot(as_bf16(above), totals)).astype(jnp.int32) - 1
    slot = rank
    local = m
    fresh_i = fresh.astype(jnp.int32)
    for o in range(1, owners):
        past = m >= o * mesh_dev
        start = jnp.sum(
            jnp.sum(jnp.where(past, 0, fresh_i), axis=0, keepdims=True), axis=1, keepdims=True
        )
        slot = jnp.where(past, rank + (o * CAP - start), slot)
        local = jnp.where(past, m - o * mesh_dev, local)
    slot_ref[...] = slot
    value = jnp.where(fresh, local + 1, 0)
    found = []
    for o in range(owners):
        places = o * CAP + lax.broadcasted_iota(jnp.int32, (CAP, LANES), 0)
        total = jnp.zeros((CAP, LANES), jnp.int32)
        for r in range(rows):
            total = total + jnp.where(slot[r : r + 1, :] == places, value[r : r + 1, :], 0)
        found.append(total)
    pad = jnp.zeros((LANES - CAP, LANES), jnp.int32)
    for o in range(owners):
        square = jnp.transpose(jnp.concatenate([found[o], pad], axis=0))
        ids_ref[o : o + 1, :] = jnp.sum(square, axis=0, keepdims=True) - 1


def node_pre_kernel(ml_ref, cot_ref, ws_ref, bn_ref, wno_ref, self_ref, cw_ref):
    self_ref[...] = dot(ml_ref[...], ws_ref[...]) + bn_ref[...]
    cw_ref[...] = dot_nt(cot_ref[...], wno_ref[...])


def hidden_kernel(gv_ref, win_ref, bin_ref, out_ref):
    v = dot(gv_ref[...], win_ref[...]) + bin_ref[...]
    out_ref[...] = (v * sigmoid(v)).astype(BF16)


def grid_kernel(ids_ref, hid_ref, wout_ref, gain_ref, ug_ref, lat_t_ref, out_ref, pg):
    @pl.when(pl.program_id(0) == 0)
    def _():
        out = dot(hid_ref[...], wout_ref[...])
        mean = jnp.mean(out, axis=-1, keepdims=True)
        centred = out - mean
        var = jnp.mean(centred * centred, axis=-1, keepdims=True)
        latent = centred * lax.rsqrt(var + 1e-05) * gain_ref[...]
        pg[...] = dot(latent.astype(BF16), ug_ref[...]).astype(BF16)
        lat_t_ref[...] = jnp.transpose(latent).astype(BF16)

    onehot = edges_by_ids(grid_block(ids_ref, pg.shape[0]), pg.shape[0], 0.5)
    out_ref[...] = dot(onehot, pg[...]).astype(BF16)


def take_latent_kernel(ids_ref, lat_t_ref, act_ref, ml_ref, out_ref, act_t_ref, ml_t_ref):
    @pl.when(pl.program_id(0) == 0)
    def _():
        act_t_ref[...] = jnp.transpose(act_ref[...])
        ml_t_ref[...] = jnp.transpose(ml_ref[...])

    onehot = ids_by_edges(grid_block(ids_ref, lat_t_ref.shape[1]), lat_t_ref.shape[1])
    out_ref[...] = dot(lat_t_ref[...], onehot).astype(BF16)


def ask_kernel(ids_ref, ml_ref, asked_ref, onehot_ref):
    owners = ids_ref.shape[0]
    nodes = ml_ref.shape[0]
    columns = jnp.transpose(ids_ref[...])
    lanes = lax.broadcasted_iota(jnp.int32, (CAP, nodes), 1)
    onehot = jnp.concatenate(
        [as_bf16(columns[:CAP, o : o + 1] == lanes) for o in range(owners)], axis=0
    )
    onehot_ref[...] = onehot
    asked_ref[...] = dot(onehot, ml_ref[...]).astype(BF16)


def half_pre(slot, pm, half_pg, bias):
    return dot(edges_by_ids(slot, pm.shape[0], 0.5), pm) + half_pg.astype(F32) + 0.5 * bias


def edge_kernel(steps, slot_ref, pg_ref, ml_ref, um_ref, be_ref, we_ref, sums_ref, act_ref, pm_ref, total):
    step = pl.program_id(0)

    @pl.when(step == 0)
    def _():
        total[...] = jnp.zeros_like(total)
        pm_ref[...] = dot(ml_ref[...], um_ref[...]).astype(BF16)

    slot = slot_ref[...]
    v = half_pre(slot, pm_ref[...], pg_ref[...], be_ref[...])
    act = (v + v * jnp.tanh(v)).astype(BF16)
    total[...] += dot(ids_by_edges(slot, total.shape[0]), act)

    @pl.when(step == steps - 1)
    def _():
        sums = total[...]
        high = sums.astype(BF16)
        low = (sums - high.astype(F32)).astype(BF16)
        act_ref[...] = high
        sums_ref[...] = (dot(high, we_ref[...]) + dot(low, we_ref[...])).astype(BF16)


def slope_kernel(slot_ref, pg_ref, pm_ref, be_ref, slope_ref, total_ref):
    @pl.when(pl.program_id(0) == 0)
    def _():
        total_ref[...] = jnp.zeros_like(total_ref)

    slot = slot_ref[...]
    v = half_pre(slot, pm_ref[...], pg_ref[...], be_ref[...])
    t = jnp.tanh(v)
    slope = ((1.0 + t) * (1.0 + v * (1.0 - t))).astype(BF16)
    slope_ref[...] = slope
    total_ref[...] += dot(ids_by_edges(slot, total_ref.shape[0]), slope)


def owned(row_ref, rec_ref, nodes):
    places = lax.broadcasted_iota(jnp.int32, (nodes, row_ref.shape[1]), 0)
    return dot(as_bf16(places == row_ref[...]), rec_ref[...]).astype(BF16)


def load(pairs, sems):
    copies = [pltpu.make_async_copy(a, b, sems.at[i]) for i, (a, b) in enumerate(pairs)]
    for copy in copies:
        copy.start()
    return copies


def node_kernel(
    rec_ref, row_ref, oh_hbm, self_hbm, cw_hbm, wa_hbm, gask_ref, gnode_ref, nact_ref,
    oh_ref, self_ref, cw_ref, wa_ref, sems,
):
    pairs = [(wa_hbm, wa_ref), (self_hbm, self_ref), (cw_hbm, cw_ref), (oh_hbm, oh_ref)]
    wa, own, cw, oh = load(pairs, sems)
    agg = owned(row_ref, rec_ref, self_ref.shape[0])
    wa.wait()
    pre = dot(agg, wa_ref[...])
    own.wait()
    pre = self_ref[...] + pre
    s = sigmoid(pre)
    cw.wait()
    g_node = (cw_ref[...] * (s * (1.0 + pre * (1.0 - s)))).astype(BF16)
    g_agg = dot_nt(g_node, wa_ref[...]).astype(BF16)
    oh.wait()
    gask_ref[...] = dot(oh_ref[...], g_agg).astype(BF16)
    gnode_ref[...] = g_node
    nact_ref[...] = (pre * s).astype(BF16)


def slot_grad_kernel(gc_ref, we_ref, slope_ref, gsum_ref, h_ref):
    h = 0.5 * dot_nt(gc_ref[...], we_ref[...])
    h_ref[...] = h.astype(BF16)
    gsum_ref[...] = (h * slope_ref[...]).astype(BF16)


def node_post_kernel(
    rec_ref, row_ref, gnode_ref, nact_ref, ml_ref, cot_ref, wno_ref, ws_ref, um_ref, mo_ref, gm_ref
):
    g_pmesh = owned(row_ref, rec_ref, ml_ref.shape[0])
    mo_ref[...] = (ml_ref[...].astype(F32) + dot(nact_ref[...], wno_ref[...])).astype(BF16)
    gm_ref[...] = (
        cot_ref[...].astype(F32) + dot_nt(gnode_ref[...], ws_ref[...]) + dot_nt(g_pmesh, um_ref[...])
    ).astype(BF16)


def put_halves(place, value, keep_ref, give_ref):
    core = lax.axis_index("core")
    half = value.shape[0] // 2

    @pl.when(core == 0)
    def _():
        keep_ref[place] = value[:half]
        give_ref[place] = value[half:]

    @pl.when(core != 0)
    def _():
        keep_ref[place] = value[half:]
        give_ref[place] = value[:half]


def edge_back_kernel(
    steps, slot_ref, slope_ref, lat_t_ref, h_ref, gsum_hbm, ml_hbm, gc_hbm, act_hbm, keep_hbm, give_hbm,
    total, gsum_ref, ml_ref, gc_ref, act_ref, keep_ref, give_ref, sems, out_sems,
):
    step = pl.program_id(0)
    late = [(act_hbm, act_ref), (gc_hbm, gc_ref), (ml_hbm, ml_ref), (gsum_hbm, gsum_ref)]

    def leaving(which):
        rows = pl.ds(1, 2) if which else pl.ds(0, 1)
        return [
            pltpu.make_async_copy(keep_ref.at[rows], keep_hbm.at[rows], out_sems.at[2 * which]),
            pltpu.make_async_copy(give_ref.at[rows], give_hbm.at[rows], out_sems.at[2 * which + 1]),
        ]

    @pl.when(step == 0)
    def _():
        total[...] = jnp.zeros_like(total)
        load(late, sems)

    onehot = edges_by_ids(slot_ref[...], h_ref.shape[0])
    g_edge = (dot(onehot, h_ref[...]) * slope_ref[...].astype(F32)).astype(BF16)
    total[...] += dot(lat_t_ref[...], g_edge)

    @pl.when(step == max(steps - 2, 0))
    def _():
        for i, (a, b) in enumerate(late):
            pltpu.make_async_copy(a, b, sems.at[i]).wait()
        put_halves(1, dot(act_ref[...], gc_ref[...]).astype(BF16), keep_ref, give_ref)
        put_halves(2, dot(ml_ref[...], gsum_ref[...]).astype(BF16), keep_ref, give_ref)
        for copy in leaving(1):
            copy.start()

    @pl.when(step == steps - 1)
    def _():
        put_halves(0, total[...].astype(BF16), keep_ref, give_ref)
        for copy in leaving(0):
            copy.start()
        for copy in leaving(1) + leaving(0):
            copy.wait()


def stage_kernel(keep_ref, out_ref):
    out_ref[...] = keep_ref[...]


def parts_kernel(keep_ref, got_ref, out_ref):
    count, _, width = out_ref.shape
    low = keep_ref.shape[1] // count
    for i in range(keep_ref.shape[0]):
        both = (keep_ref[i].astype(F32) + got_ref[i].astype(F32)).astype(BF16)
        out_ref[:, i * low : (i + 1) * low] = both.reshape(count, low, width)


def spread_kernel(scale, parts_ref, out_ref):
    total = (jnp.sum(parts_ref[...].astype(F32), axis=0) * scale).astype(BF16)
    out_ref[...] = jnp.broadcast_to(total[None], out_ref.shape)


def finish_kernel(ours, part_ref, *refs):
    *out_refs, rows_ref, sems = refs[-5:]
    count, rows, width = part_ref.shape
    low = rows // len(out_refs)
    half = count * low
    core = lax.axis_index("core")
    start = pl.multiple_of((core if ours else 1 - core) * half, half)
    copies = []
    for i, out_ref in enumerate(out_refs):
        piece = part_ref[:, i * low : (i + 1) * low]
        rows_ref[i] = piece.astype(F32).reshape(half, width)
        copies.append(pltpu.make_async_copy(rows_ref.at[i], out_ref.at[pl.ds(start, half)], sems.at[i]))
        copies[i].start()
    for copy in copies:
        copy.wait()


def finish(ours, part, width, before=()):
    anywhere = pl.BlockSpec(memory_space=pl.ANY)
    half = width // 2
    return pl.pallas_call(
        functools.partial(finish_kernel, ours),
        out_shape=[jax.ShapeDtypeStruct((width, width), F32)] * 3,
        in_specs=[pl.BlockSpec(memory_space=pltpu.VMEM)] + [anywhere] * len(before),
        out_specs=[anywhere] * 3,
        scratch_shapes=[pltpu.VMEM((3, half, width), F32), pltpu.SemaphoreType.DMA((3,))],
        input_output_aliases={i + 1: i for i in range(len(before))},
        name="finish_ours" if ours else "finish_other",
        cost_estimate=pl.CostEstimate(flops=3 * half * width, bytes_accessed=18 * half * width, transcendentals=0),
        compiler_params=pltpu.CompilerParams(vmem_limit_bytes=16 << 20),
    )(part, *before)


def other_core(value):
    return lax.ppermute(value, "core", [(0, 1), (1, 0)])


def held(value, after):
    def body(*refs):
        pass

    anywhere = pl.BlockSpec(memory_space=pl.ANY)
    return pl.pallas_call(
        body,
        out_shape=jax.ShapeDtypeStruct(value.shape, value.dtype),
        in_specs=[anywhere] * (1 + len(after)),
        out_specs=anywhere,
        input_output_aliases={0: 0},
        name="held",
        compiler_params=pltpu.CompilerParams(vmem_limit_bytes=60 << 20),
    )(value, *after)


def shards(
    grid_vars,
    mesh_latent,
    cotangent,
    edge_grid,
    edge_mesh,
    w_in,
    b_in,
    w_out,
    norm_gain,
    u_grid,
    u_mesh,
    b_edge,
    w_edge,
    w_self,
    w_agg,
    b_node,
    w_node_out,
):
    grid_dev, variables = grid_vars.shape
    mesh_dev, width = mesh_latent.shape
    edge_dev = edge_grid.shape[0]
    owners = lax.axis_size("mesh")
    slots = owners * CAP
    rows = edge_dev // LANES
    block = ROWS * LANES
    steps = edge_dev // block
    scale = (edge_dev * lax.axis_size("x") * lax.axis_size("core") * owners) ** (-0.5)
    sds, hbm = jax.ShapeDtypeStruct, pltpu.HBM

    def exchange(value):
        return lax.all_to_all(value, "mesh", 0, 0, tiled=True)

    grid_ids = edge_grid.reshape(rows, LANES)
    slot, ids = call(
        functools.partial(prep_kernel, owners, mesh_dev),
        "prep",
        [sds((rows, LANES), jnp.int32), sds((owners, LANES), jnp.int32)],
        [edge_mesh.reshape(rows, LANES)],
        1e9,
        vmem=60,
    )
    incoming = exchange(ids)

    tile = min(256, grid_dev)
    grid_spec = pl.BlockSpec((tile, width), lambda i: (i, 0))
    hidden, hidden_done = call(
        hidden_kernel,
        "hidden",
        [hbm((grid_dev, width), BF16)],
        [grid_vars, w_in, b_in.reshape(1, width)],
        2 * grid_dev * width * variables,
        grid=(grid_dev // tile,),
        in_specs=[
            pl.BlockSpec((tile, variables), lambda i: (i, 0)),
            whole((variables, width)),
            whole((1, width)),
        ],
        out_specs=[grid_spec],
        after=[slot],
        token=True,
    )

    node_f, node_b = hbm((mesh_dev, width), F32), hbm((mesh_dev, width), BF16)
    self_part, cot_part, node_pre_done = call(
        node_pre_kernel,
        "node_pre",
        [node_f, node_f],
        [mesh_latent, cotangent, w_self, b_node.reshape(1, width), w_node_out],
        4 * mesh_dev * width * width,
        vmem=52,
        after=[hidden_done],
        token=True,
    )
    asked, onehot_in = call(
        ask_kernel,
        "ask",
        [sds((slots, width), BF16), sds((slots, mesh_dev), BF16)],
        [incoming, mesh_latent],
        2 * slots * mesh_dev * width,
        after=[node_pre_done],
    )
    incoming_row = incoming[:, :CAP].reshape(1, slots)
    slot_latent = exchange(asked)

    id_spec = pl.BlockSpec((ROWS, LANES), lambda i: (i, 0))
    edge_spec = pl.BlockSpec((block, width), lambda i: (i, 0))
    edge_t_spec = pl.BlockSpec((width, block), lambda i: (0, i))
    latent_t, edge_pgrid = call(
        grid_kernel,
        "grid",
        [sds((width, grid_dev), BF16), sds((edge_dev, width), BF16)],
        [grid_ids, hidden, w_out, norm_gain.reshape(1, width), u_grid],
        4 * grid_dev * width * width + 2 * edge_dev * grid_dev * width,
        grid=(steps,),
        in_specs=[
            id_spec, whole((grid_dev, width)), whole((width, width)), whole((1, width)),
            whole((width, width)),
        ],
        out_specs=[whole((width, grid_dev)), edge_spec],
        scratch=[pltpu.VMEM((grid_dev, width), BF16)],
        vmem=60,
        after=[asked],
    )

    slots_b, slots_h = sds((slots, width), BF16), hbm((slots, width), BF16)
    slots_spec = whole((slots, width))
    mesh_spec = whole((mesh_dev, width))
    weight_spec = whole((width, width))
    row_spec = whole((1, slots))
    bias = b_edge.reshape(1, width)
    sums, act_sums, slot_pmesh = call(
        functools.partial(edge_kernel, steps),
        "edge",
        [slots_b, slots_h, slots_h],
        [slot, edge_pgrid, slot_latent, u_mesh, bias, w_edge],
        4 * edge_dev * slots * width + 6 * slots * width * width,
        grid=(steps,),
        in_specs=[id_spec, edge_spec, slots_spec, weight_spec, whole((1, width)), weight_spec],
        out_specs=[slots_spec, slots_spec, slots_spec],
        scratch=[pltpu.VMEM((slots, width), F32)],
        vmem=52,
    )
    received = exchange(sums)

    slope, slope_sums = call(
        slope_kernel,
        "slope",
        [hbm((edge_dev, width), BF16), hbm((slots, width), F32)],
        [slot, edge_pgrid, slot_pmesh, bias],
        4 * edge_dev * slots * width,
        grid=(steps,),
        in_specs=[id_spec, edge_spec, slots_spec, whole((1, width))],
        out_specs=[edge_spec, slots_spec],
        vmem=60,
        after=[sums],
    )
    g_asked, g_node, node_act = call(
        node_kernel,
        "node",
        [slots_b, node_b, node_b],
        [received, incoming_row, onehot_in, self_part, cot_part, w_agg],
        4 * mesh_dev * width * width + 4 * mesh_dev * slots * width,
        in_specs=[pl.BlockSpec(memory_space=pltpu.VMEM)] * 2 + [pl.BlockSpec(memory_space=pl.ANY)] * 4,
        scratch=[
            pltpu.VMEM((slots, mesh_dev), BF16),
            pltpu.VMEM((mesh_dev, width), F32),
            pltpu.VMEM((mesh_dev, width), F32),
            pltpu.VMEM((width, width), BF16),
            pltpu.SemaphoreType.DMA((4,)),
        ],
        vmem=52,
        after=[slope],
    )
    slot_g = exchange(g_asked)

    slots_t_spec = whole((width, slots))
    edge_latent_t, act_sums_t, slot_latent_t, take_done = call(
        take_latent_kernel,
        "take_latent",
        [hbm((width, edge_dev), BF16), hbm((width, slots), BF16), hbm((width, slots), BF16)],
        [grid_ids, latent_t, act_sums, slot_latent],
        2 * edge_dev * grid_dev * width,
        grid=(steps,),
        in_specs=[id_spec, whole((width, grid_dev)), slots_spec, slots_spec],
        out_specs=[edge_t_spec, slots_t_spec, slots_t_spec],
        vmem=52,
        after=[g_asked],
        token=True,
    )
    half = width // 2
    gsum, h = call(
        slot_grad_kernel,
        "slot_grad",
        [slots_h, slots_h],
        [slot_g, w_edge, slope_sums],
        2 * slots * width * width,
        vmem=52,
        after=[take_done],
    )
    gsum_received = exchange(gsum)

    three = hbm((3, half, width), BF16)
    keep, give = call(
        functools.partial(edge_back_kernel, steps),
        "edge_back",
        [three, three],
        [slot, slope, edge_latent_t, h, gsum, slot_latent_t, slot_g, act_sums_t],
        2 * edge_dev * (slots + width) * width + 4 * slots * width * width,
        grid=(steps,),
        in_specs=[id_spec, edge_spec, edge_t_spec, slots_spec] + [pl.BlockSpec(memory_space=pl.ANY)] * 4,
        out_specs=[pl.BlockSpec(memory_space=pl.ANY)] * 2,
        scratch=[pltpu.VMEM((width, width), F32)]
        + [pltpu.VMEM(a, BF16) for a in ((slots, width), (width, slots)) * 2]
        + [pltpu.VMEM((3, half, width), BF16)] * 2
        + [pltpu.SemaphoreType.DMA((4,))] * 2,
        vmem=60,
    )
    others = ("mesh", "x")
    count = lax.axis_size("x") * owners
    pieces = sds((count, 3 * half // count, width), BF16)
    (staged,) = call(stage_kernel, "stage", [sds((3, half, width), BF16)], [keep], half * width)
    (parts,) = call(
        parts_kernel,
        "parts",
        [pieces],
        [staged, other_core(held(give, [gsum_received]))],
        3 * half * width,
    )
    summed = lax.all_to_all(parts, others, 0, 0, tiled=True)

    mesh_out, grad_mesh, node_post_done = call(
        node_post_kernel,
        "node_post",
        [node_b, node_b],
        [
            gsum_received, incoming_row, g_node, node_act, mesh_latent, cotangent,
            w_node_out, w_self, u_mesh,
        ],
        6 * mesh_dev * width * width + 2 * mesh_dev * slots * width,
        vmem=52,
        after=[parts],
        token=True,
    )
    (copies,) = call(
        functools.partial(spread_kernel, scale),
        "spread",
        [pieces],
        [summed],
        3 * half * width,
        after=[node_post_done],
    )
    mine = lax.all_to_all(copies, others, 0, 0, tiled=True)
    other = other_core(mine)
    grad_ugrid, grad_edge, grad_umesh = finish(False, other, width, finish(True, mine, width))
    return mesh_out, grad_mesh, grad_edge, grad_ugrid, grad_umesh


def solution(mesh):
    bands, owners = mesh.shape["band"], mesh.shape["mesh"]
    cores = 2
    fine = Mesh(mesh.devices.reshape(bands // cores, cores, owners), ("x", "core", "mesh"))
    split = ("x", "core", "mesh")
    return jax.shard_map(
        shards,
        mesh=fine,
        in_specs=(P(split, None),) * 3 + (P(split),) * 2 + (P(),) * 12,
        out_specs=(P(split, None), P(split, None), P(), P(), P()),
        check_vma=False,
    )
```
